32 devices in a mesh: az: 4 (over x, core), rg: 8 (over z, y).
Axes of the slice: x: 2, y: 2, z: 4, core: 2. Of those that a mesh axis runs over, the one named last changes fastest.
Arguments:
- reference_image: bfloat16 [2, 512, 2048], P(None, 'az', 'rg'), may hold values from -600 to 600, as said below
- secondary_image: bfloat16 [2, 512, 2048], P(None, 'az', 'rg'), may hold values from -600 to 600, as said below
- block_shifts: int32 [2, 8, 32], P(None, 'az', 'rg'), may hold values from -8 to 8
- shift_bins: int32 [2, 8, 32], P(None, 'az', 'rg'), may hold values from 0 to 15
- land_mask: int32 [8, 32], P('az', 'rg'), may hold values from 0 to 1, as said below
- coarse_peaks: int32 [2, 8, 32], P(None, 'az', 'rg'), may hold values from -29 to 27
Outputs:
- correlation_surface: float32 [8, 32, 4096], P('az', 'rg')
- peak_patch: float32 [8, 32, 1024], P('az', 'rg')
The draws below stay inside these ranges and needn't reach their ends.
Inputs may be any that keep to these rules, and one draw needn't show every extreme that they name: `reference_image`: real and imaginary parts of a radar scene, magnitudes at most 600. `secondary_image`: the same scene seen a second time, magnitudes at most 600. `land_mask`: the share of land chips varies from tile to tile (a tile is the 2 x 4 chips of one device), and at least one tile is all land.
All inputs are finite; a program needn't handle non-finite values.
Results may differ from the reference program's by a relative error of at most 0.013.
Values may be sent and summed in bfloat16 or wider, within the bound.
A program may use at most 64 MiB of HBM per device.

```python
import math
import jax
import jax.numpy as jnp
from jax import lax

CA_DEV = 2
CR_DEV = 4
CHIP = 64
SEARCH = 32
SHIFT = 8
TAPS = 8
NBIN = 16
OVERS = 16
PATCH = 8
REACH = 12
NCA = 8
NCR = 32
NA = 512
NR = 2048


def scene_fields(key):
    base_key = jax.random.fold_in(key, 7001)
    key_list = jax.random.split(base_key, 4)
    field_shape = (2, NA, NR)
    scene_base = jax.random.truncated_normal(key_list[0], -4.0, 4.0, field_shape, jnp.float32)
    speckle_noise = jax.random.truncated_normal(key_list[1], -4.0, 4.0, field_shape, jnp.float32)
    row_scale = jnp.exp(math.log(10.0) * jax.random.uniform(key_list[2], (NA,), jnp.float32))
    column_scale = jnp.exp(math.log(10.0) * jax.random.uniform(key_list[3], (NR,), jnp.float32))
    field_scale = row_scale[:, None] * column_scale[None, :]
    first_look = scene_base * field_scale[None]
    second_look = (0.8 * scene_base + 0.6 * speckle_noise) * field_scale[None]
    return (first_look, second_look)


def draw_reference_image(key, part):
    return scene_fields(key)[0].astype(jnp.bfloat16)


def draw_secondary_image(key, part):
    return scene_fields(key)[1].astype(jnp.bfloat16)


def draw_land_mask(key, part):
    key_list = jax.random.split(jax.random.fold_in(key, 7002), 4)
    tile_rows = NCA // CA_DEV
    tile_columns = NCR // CR_DEV
    level = jax.random.randint(key_list[0], (tile_rows, tile_columns), 0, 9)
    full_row = jax.random.randint(key_list[1], (), 0, tile_rows)
    full_column = jax.random.randint(key_list[2], (), 0, tile_columns)
    chosen = (jnp.arange(tile_rows)[:, None] == full_row) & (jnp.arange(tile_columns)[None, :] == full_column)
    level = jnp.where(chosen, 8, level)
    level = jnp.repeat(jnp.repeat(level, CA_DEV, axis=0), CR_DEV, axis=1)
    dice_roll = jax.random.randint(key_list[3], (NCA, NCR), 0, 8)
    return (dice_roll < level).astype(jnp.int32)


def place_ends(result, rng, low, largest):
    spot = [jax.random.randint(jax.random.fold_in(rng, axis), (), 0, length) for axis, length in enumerate(result.shape)]
    main_axis = result.shape.index(max(result.shape))
    neighbour = spot[:main_axis] + [(spot[main_axis] + 1) % result.shape[main_axis]] + spot[main_axis + 1:]
    return result.at[tuple(spot)].set(low).at[tuple(neighbour)].set(largest)


def setup_inputs(seed: int = 0) -> dict:
    keys = jax.random.split(jax.random.key(seed), 7)
    return {
        "reference_image": draw_reference_image(jax.random.fold_in(keys[6], 71), 0),
        "secondary_image": draw_secondary_image(jax.random.fold_in(keys[6], 71), 0),
        "block_shifts": place_ends(jax.random.randint(keys[2], (2, NCA, NCR), -SHIFT, SHIFT + 1), jax.random.fold_in(keys[2], 1), -SHIFT, SHIFT).astype(jnp.int32),
        "shift_bins": place_ends(jax.random.randint(keys[3], (2, NCA, NCR), 0, NBIN), jax.random.fold_in(keys[3], 1), 0, NBIN - 1).astype(jnp.int32),
        "land_mask": draw_land_mask(jax.random.fold_in(keys[6], 71), 0),
        "coarse_peaks": place_ends(jax.random.randint(keys[5], (2, NCA, NCR), -SEARCH + PATCH // 2 - 1, SEARCH - PATCH // 2), jax.random.fold_in(keys[5], 1), -SEARCH + PATCH // 2 - 1, (SEARCH - PATCH // 2) - 1).astype(jnp.int32),
    }


epsilon = 1e-06

def lanczos(offset):
    half_taps = TAPS // 2
    inside = jnp.abs(offset) < half_taps
    return jnp.where(inside, jnp.sinc(offset) * jnp.sinc(offset / half_taps), 0.0)

def kernel_table():
    fraction = jnp.arange(NBIN).astype(jnp.float32) / NBIN
    tap_index = jnp.arange(TAPS).astype(jnp.float32)
    offset = tap_index[None, :] - (TAPS // 2 - 1) - fraction[:, None]
    return lanczos(offset).astype(jnp.bfloat16)

def patch_table():
    sample_at = (jnp.arange(2 * OVERS).astype(jnp.float32) - OVERS) / OVERS
    node_at = jnp.arange(PATCH).astype(jnp.float32) - (PATCH // 2 - 1)
    return lanczos(sample_at[:, None] - node_at[None, :]).astype(jnp.float32)

def kernel_rows(kernel, bin_index):
    matches = bin_index[:, None, None] == jnp.arange(NBIN)[None, :, None]
    return lax.optimization_barrier(jnp.sum(jnp.where(matches, kernel.astype(jnp.float32)[None], 0.0), axis=1))

def band_matrix(taps_rows):
    offset = jnp.arange(CHIP + TAPS)[None, :] - jnp.arange(CHIP)[:, None] - 1
    running = jnp.zeros((taps_rows.shape[0], CHIP, CHIP + TAPS), jnp.float32)
    for tap_index in range(TAPS):
        running = running + jnp.where(offset[None] == tap_index, taps_rows[:, tap_index][:, None, None], 0.0)
    return running.astype(jnp.bfloat16)

def resample_blocks(source, kernel, start_rows, start_columns, bin_rows, bin_columns):

    def cut_out(row_start, column_start):
        zero_index = jnp.zeros((), jnp.int32)
        return lax.dynamic_slice(source, (zero_index, row_start, column_start), (2, CHIP + TAPS, CHIP + TAPS))
    stacked = jax.vmap(cut_out)(start_rows, start_columns)
    band_rows = band_matrix(kernel_rows(kernel, bin_rows))
    band_columns = band_matrix(kernel_rows(kernel, bin_columns))
    half_done = jnp.einsum('bij,bcjk->bcik', band_rows.astype(jnp.float32), stacked.astype(jnp.float32)).astype(jnp.bfloat16)
    second = jnp.einsum('bcik,blk->bcil', half_done.astype(jnp.float32), band_columns.astype(jnp.float32))
    return jnp.sqrt(second[:, 0] * second[:, 0] + second[:, 1] * second[:, 1]).astype(jnp.bfloat16)

def normalized_correlation(chip_data, window_data):
    chip_float = chip_data.astype(jnp.float32)
    centred_low = (chip_float - lax.optimization_barrier(jnp.mean(chip_float, axis=(1, 2), keepdims=True))).astype(jnp.bfloat16)
    centred = lax.optimization_barrier(centred_low).astype(jnp.float32)
    energy = lax.optimization_barrier(jnp.sum(centred * centred, axis=(1, 2)))
    window_float = window_data.astype(jnp.float32)
    lag_index = jnp.arange(CHIP)
    hankel = window_float[:, lag_index[:, None] + lag_index[None, :], :]
    column_index = jnp.arange(2 * CHIP)
    column_gap = column_index[None, :] - lag_index[:, None]
    spread = jnp.pad(centred, ((0, 0), (0, 0), (0, CHIP)))
    toeplitz = spread[:, :, jnp.where((column_gap >= 0) & (column_gap < CHIP), column_gap, CHIP)]
    product_sum = jnp.einsum('gaiq,gidq->gad', hankel, toeplitz, precision=lax.Precision.HIGHEST)
    ones_band = ((column_index[None, :] >= lag_index[:, None]) & (column_index[None, :] < lag_index[:, None] + CHIP)).astype(jnp.float32)
    both_terms = jnp.stack([window_float, window_float * window_float], axis=1)
    row_sums = jnp.einsum('ap,gspq->gsaq', ones_band, both_terms, precision=lax.Precision.HIGHEST)
    box_sums = jnp.einsum('gsaq,dq->gsad', row_sums, ones_band, precision=lax.Precision.HIGHEST)
    window_sum = box_sums[:, 0]
    squares = box_sums[:, 1]
    chip_area = CHIP * CHIP
    return product_sum / jnp.sqrt(energy[:, None, None] * (squares - window_sum * window_sum / chip_area) + epsilon)

def oversample(surface, peak_pair, lobes):
    lead_offset = PATCH // 2 - 1
    start_rows = (peak_pair[0] + SEARCH - lead_offset).astype(jnp.int32)
    start_columns = (peak_pair[1] + SEARCH - lead_offset).astype(jnp.int32)

    def cut_patch(field_plane, row_start, column_start):
        return lax.dynamic_slice(field_plane, (row_start, column_start), (PATCH, PATCH))
    nearby = jax.vmap(cut_patch)(surface, start_rows, start_columns)
    patch_values = jnp.einsum('tk,gkl,ul->gtu', lobes, nearby, lobes, precision=lax.Precision.HIGHEST)
    return patch_values.reshape(surface.shape[0], 4 * OVERS * OVERS)

def reference(reference_image, secondary_image, block_shifts, shift_bins, land_mask, coarse_peaks):
    kernel = kernel_table()
    padded = jnp.pad(secondary_image, ((0, 0), (REACH, REACH), (REACH, REACH)))
    row_index = jnp.arange(NCA).astype(jnp.int32)
    column_base = (jnp.arange(NCR) * CHIP + REACH - TAPS // 2).astype(jnp.int32)

    def resample_row(chip_row):
        shift_pair = block_shifts[:, chip_row]
        bin_pair = shift_bins[:, chip_row]
        start_rows = (chip_row * CHIP + REACH - TAPS // 2 + shift_pair[0]).astype(jnp.int32)
        start_columns = (column_base + shift_pair[1]).astype(jnp.int32)
        blocks = resample_blocks(padded, kernel, start_rows, start_columns, bin_pair[0], bin_pair[1])
        return blocks.transpose(1, 0, 2).reshape(CHIP, NR)
    amplitude = lax.map(resample_row, row_index).reshape(NA, NR)
    extended = jnp.pad(amplitude, SEARCH)
    reference_float = reference_image.astype(jnp.float32)
    reference_amplitude = jnp.sqrt(reference_float[0] * reference_float[0] + reference_float[1] * reference_float[1]).astype(jnp.bfloat16)
    lobes = patch_table()
    group_size = 8

    def correlate_group(group_pair):
        return normalized_correlation(group_pair[0], group_pair[1])

    def correlate_row(chip_row):
        strip = lax.dynamic_slice_in_dim(reference_amplitude, chip_row * CHIP, CHIP, 0)
        chip_data = strip.reshape(CHIP, NCR, CHIP).transpose(1, 0, 2)
        window_strip = lax.dynamic_slice_in_dim(extended, chip_row * CHIP, 2 * CHIP, 0)
        pieces = window_strip.reshape(2 * CHIP, NCR + 1, CHIP)
        window_data = jnp.concatenate([pieces[:, :-1], pieces[:, 1:]], axis=2).transpose(1, 0, 2)
        grouped = lax.map(correlate_group, (chip_data.reshape(NCR // group_size, group_size, CHIP, CHIP), window_data.reshape(NCR // group_size, group_size, 2 * CHIP, 2 * CHIP)))
        surface = grouped.reshape(NCR, CHIP, CHIP)
        surface = jnp.where(land_mask[chip_row][:, None, None] == 1, surface, 0.0)
        patch_values = oversample(surface, coarse_peaks[:, chip_row], lobes)
        return (surface.reshape(NCR, CHIP * CHIP), patch_values)
    surface, patch_values = lax.map(correlate_row, row_index)
    return (surface, patch_values)
```

```python
import jax
import jax.numpy as jnp
import ml_dtypes
import numpy as np
from jax import lax
from jax.experimental import pallas as pl
from jax.experimental.pallas import tpu as pltpu
from jax.sharding import PartitionSpec as P

CHIP = 64
SEARCH = 32
TAPS = 8
NBIN = 16
OVERS = 16
PATCH = 8
LINES = 48
COLS = 128
GROUP = 8
EPSILON = 1e-06
F32, BF16 = jnp.float32, jnp.bfloat16


def lanczos(x):
    return np.where(np.abs(x) < 4, np.sinc(x) * np.sinc(x / 4), 0.0)


def tap_table():
    taps = lanczos(np.arange(TAPS)[None, :] - 3 - np.arange(NBIN)[:, None] / NBIN)
    taps = taps.astype(np.float32).astype(ml_dtypes.bfloat16).astype(np.float32)
    return np.concatenate([np.zeros((1, TAPS), np.float32), taps]).reshape(-1)


def lobe_table():
    at = (np.arange(2 * OVERS) - OVERS) / OVERS
    lobes = lanczos(at[:, None] - (np.arange(PATCH) - (PATCH // 2 - 1))[None, :])
    return np.pad(lobes.astype(np.float32), ((0, 0), (0, 128 - PATCH)))


def with_halo(cells, axis, dim, width):
    count = lax.axis_size(axis)
    head = lax.slice_in_dim(cells, 0, width, axis=dim)
    tail = lax.slice_in_dim(cells, cells.shape[dim] - width, cells.shape[dim], axis=dim)
    up = [(i, i + 1) for i in range(count - 1)]
    down = [(i + 1, i) for i in range(count - 1)]
    return jnp.concatenate(
        [lax.ppermute(tail, axis, up), cells, lax.ppermute(head, axis, down)], axis=dim
    )


def dot_nt(a, b, **kw):
    return lax.dot_general(a, b, (((1,), (1,)), ((), ())), preferred_element_type=F32, **kw)


def split3(x):
    hi = x.astype(BF16)
    rest = x - hi.astype(F32)
    mid = rest.astype(BF16)
    return hi, mid, (rest - mid.astype(F32)).astype(BF16)


def band(rows, span, base, tab, par, shift_at, bin_at):
    gap = lax.broadcasted_iota(jnp.int32, (rows, span), 1) - lax.broadcasted_iota(
        jnp.int32, (rows, span), 0
    )
    gap = gap - (base - (TAPS // 2 - 1) + par[shift_at])
    f = par[bin_at]
    out = jnp.zeros((rows, span), F32)
    for t in range(TAPS):
        out = jnp.where(gap == t, tab[f * TAPS + t], out)
    return out.astype(BF16)


def body(
    nu, nv, par, tab, mask, peaks, ext, ref, lobes, out, patch, amp, win, cen, wts, toep, tmp, tmp2,
    flat, flat2,
):
    chunks = (nv * CHIP + 2 * SEARCH + 127) // 128
    mu, mv = nu + 2, nv + 2
    for u in range(-1, nu + 1):
        rows = CHIP if 0 <= u < nu else SEARCH
        first = u * CHIP + (CHIP - SEARCH if u < 0 else 0)
        low = (first + LINES - 12) // 16 * 16
        high = min(-(-(first + LINES + rows + 12) // 16) * 16, nu * CHIP + 2 * LINES)
        totals = [None] * chunks
        for v in range(-1, nv + 1):
            at = (u + 1) * mv + v + 1
            begin = max(v * CHIP, -SEARCH)
            end = min(v * CHIP + CHIP, nv * CHIP + SEARCH)
            left = (begin + COLS - 12) // 128 * 128
            right = left + 256
            a = band(rows, high - low, first + LINES - low, tab, par, at, 2 * mu * mv + at)
            half = jnp.concatenate(
                [
                    jnp.dot(a, ext[c, low:high, left:right], preferred_element_type=F32)
                    for c in range(2)
                ],
                axis=0,
            ).astype(BF16)
            b = band(
                end - begin, 256, begin + COLS - left, tab, par, mu * mv + at, 3 * mu * mv + at
            )
            spot = begin + SEARCH
            while spot < end + SEARCH:
                m = spot // 128
                stop = min(end + SEARCH, (m + 1) * 128)
                part = b[spot - SEARCH - begin : stop - SEARCH - begin]
                pieces = [part]
                if spot > m * 128:
                    pieces.insert(0, jnp.zeros((spot - m * 128, 256), BF16))
                if stop < m * 128 + 128:
                    pieces.append(jnp.zeros((m * 128 + 128 - stop, 256), BF16))
                piece = jnp.concatenate(pieces, axis=0) if len(pieces) > 1 else part
                term = dot_nt(half, piece)
                totals[m] = term if totals[m] is None else totals[m] + term
                spot = stop
        for m in range(chunks):
            re, im = totals[m][:rows], totals[m][rows:]
            amp[first + SEARCH : first + SEARCH + rows, m * 128 : m * 128 + 128] = (
                jnp.sqrt(re * re + im * im).astype(BF16).astype(F32)
            )

    lane = lax.broadcasted_iota(jnp.int32, (2 * CHIP, 128), 1)
    low_lanes = lane < CHIP
    re = ref[0].astype(F32)
    im = ref[1].astype(F32)
    across = jnp.sqrt(re * re + im * im).astype(BF16).astype(F32).T
    for u in range(nu):
        for v in range(nv):
            n = u * nv + v
            lines = slice(u * CHIP, u * CHIP + 2 * CHIP)
            m = v // 2
            if v % 2 == 0:
                win[n] = amp[lines, m * 128 : m * 128 + 128]
            else:
                win[n] = jnp.where(
                    low_lanes,
                    pltpu.roll(amp[lines, m * 128 : m * 128 + 128], 64, 1),
                    pltpu.roll(amp[lines, m * 128 + 128 : m * 128 + 256], 64, 1),
                )
            wide = u // 2 * 128
            chip = across[v * CHIP : v * CHIP + CHIP, wide : wide + 128]
            if u % 2:
                chip = pltpu.roll(chip, 64, 1)
            keep = low_lanes[:CHIP]
            chip = jnp.where(keep, chip, 0.0)
            mean = jnp.sum(jnp.sum(chip, axis=1, keepdims=True), axis=0, keepdims=True)
            mean = mean * (1.0 / (CHIP * CHIP))
            cen[n] = jnp.where(keep, (chip - mean).astype(BF16).astype(F32), 0.0)

    gap_r = lax.broadcasted_iota(jnp.int32, (CHIP, 128), 1) - lax.broadcasted_iota(
        jnp.int32, (CHIP, 128), 0
    )
    ones_r = jnp.where((gap_r >= 0) & (gap_r < CHIP), 1.0, 0.0).astype(BF16)
    gap_c = lax.broadcasted_iota(jnp.int32, (128, 128), 0) - lane
    ones_c = jnp.where((gap_c >= 0) & (gap_c < CHIP), 1.0, 0.0).astype(BF16)

    def one_chip(n, carry):
        w = win[n]
        for s in range(GROUP):
            shifted = pltpu.roll(w, 128 - s, 1) if s else w
            wts[s * 128 : s * 128 + 128, :] = shifted.astype(BF16)
        centred = cen[n]
        for j in range(CHIP):
            k, s = j // GROUP, j % GROUP
            line = jnp.broadcast_to(centred[j : j + 1, :], (CHIP, 128))
            toep[k * CHIP : k * CHIP + CHIP, s * 128 : s * 128 + 128] = pltpu.roll(
                line, 0, 1, stride=1, stride_axis=0
            ).astype(BF16)
        prod = jnp.dot(toep[...], wts[...], preferred_element_type=F32)
        cross = prod[:CHIP]
        for k in range(1, CHIP // GROUP):
            cross = cross + pltpu.roll(prod[k * CHIP : k * CHIP + CHIP], 128 - k * GROUP, 1)
        energy = jnp.sum(jnp.sum(centred * centred, axis=1, keepdims=True), axis=0, keepdims=True)
        square = w * w
        square_hi = square.astype(BF16)
        square_lo = (square - square_hi.astype(F32)).astype(BF16)
        sums = jnp.dot(
            ones_r,
            jnp.concatenate([w.astype(BF16), square_hi, square_lo], axis=1),
            preferred_element_type=F32,
        )
        terms = split3(sums[:, :128]) + split3(sums[:, 128:256] + sums[:, 256:])
        boxes = jnp.dot(jnp.concatenate(terms, axis=0), ones_c, preferred_element_type=F32)
        box = [boxes[i * CHIP : i * CHIP + CHIP] for i in range(6)]
        total = box[2] + box[1] + box[0]
        squares = box[5] + box[4] + box[3]
        normed = cross / jnp.sqrt(
            energy * (squares - total * total * (1.0 / (CHIP * CHIP))) + EPSILON
        )
        land = (mask[n] == 1) & low_lanes[:CHIP]
        surface = jnp.where(land, normed, 0.0)
        tmp[...] = surface
        pairs = tmp[pl.ds(0, 32, stride=2), :] + pltpu.roll(tmp[pl.ds(1, 32, stride=2), :], 64, 1)
        flat[n] = pairs
        lead = SEARCH - (PATCH // 2 - 1)
        lobe_a = pltpu.roll(lobes[...], peaks[n] + lead, 1)
        lobe_d = pltpu.roll(lobes[...], peaks[nu * nv + n] + lead, 1)
        near = jnp.dot(
            lobe_a,
            jnp.concatenate([surface, jnp.zeros((CHIP, 128), F32)], axis=0),
            preferred_element_type=F32,
            precision=lax.Precision.HIGHEST,
        )
        tall = jnp.concatenate([lobe_d, jnp.zeros((96, 128), F32)], axis=0)
        tmp2[...] = dot_nt(near, tall, precision=lax.Precision.HIGHEST)
        quads = tmp2[pl.ds(0, 8, stride=4), :]
        for r in range(1, 4):
            quads = quads + pltpu.roll(tmp2[pl.ds(r, 8, stride=4), :], 32 * r, 1)
        flat2[n] = quads
        return carry

    lax.fori_loop(0, nu * nv, one_chip, 0)
    for u in range(nu):
        for v in range(nv):
            for m in range(CHIP // 2):
                out[u, v : v + 1, m * 128 : m * 128 + 128] = flat[u * nv + v, m : m + 1, :]
            for m in range(8):
                patch[u, v : v + 1, m * 128 : m * 128 + 128] = flat2[u * nv + v, m : m + 1, :]


def per_device(reference_image, secondary_image, block_shifts, shift_bins, land_mask, coarse_peaks):
    nu, nv = land_mask.shape
    par = jnp.concatenate([block_shifts, shift_bins + 1], axis=0)
    par = with_halo(with_halo(par, "az", 1, 1), "rg", 2, 1)
    ext = with_halo(with_halo(secondary_image, "az", 1, LINES), "rg", 2, COLS)
    smem = pl.BlockSpec(memory_space=pltpu.SMEM)
    vmem = pl.BlockSpec(memory_space=pltpu.VMEM)
    n = nu * nv
    chunks = (nv * CHIP + 2 * SEARCH + 127) // 128

    def kernel(*refs):
        body(nu, nv, *refs)

    return pl.pallas_call(
        kernel,
        out_shape=(
            jax.ShapeDtypeStruct((nu, nv, CHIP * CHIP), F32),
            jax.ShapeDtypeStruct((nu, nv, 4 * OVERS * OVERS), F32),
        ),
        in_specs=[smem] * 4 + [vmem] * 3,
        out_specs=(vmem, vmem),
        scratch_shapes=[
            pltpu.VMEM((nu * CHIP + 2 * SEARCH, chunks * 128), F32),
            pltpu.VMEM((n, 2 * CHIP, 128), F32),
            pltpu.VMEM((n, CHIP, 128), F32),
            pltpu.VMEM((GROUP * 128, 128), BF16),
            pltpu.VMEM((CHIP * CHIP // GROUP, GROUP * 128), BF16),
            pltpu.VMEM((CHIP, 128), F32),
            pltpu.VMEM((2 * OVERS, 128), F32),
            pltpu.VMEM((n, CHIP // 2, 128), F32),
            pltpu.VMEM((n, 8, 128), F32),
        ],
        compiler_params=pltpu.CompilerParams(vmem_limit_bytes=48 * 1024 * 1024),
    )(
        par.reshape(-1),
        jnp.asarray(tap_table()),
        land_mask.reshape(-1),
        coarse_peaks.reshape(-1),
        ext,
        reference_image,
        jnp.asarray(lobe_table()),
    )


def solution(mesh):
    cut = P(None, "az", "rg")
    return jax.shard_map(
        per_device,
        mesh=mesh,
        in_specs=(cut, cut, cut, cut, P("az", "rg"), cut),
        out_specs=(P("az", "rg", None), P("az", "rg", None)),
        check_vma=False,
    )
```

```python
import jax
import jax.numpy as jnp
import ml_dtypes
import numpy as np
from jax import lax
from jax.experimental import pallas as pl
from jax.experimental.pallas import tpu as pltpu
from jax.sharding import PartitionSpec as P

CHIP = 64
SEARCH = 32
TAPS = 8
NBIN = 16
OVERS = 16
PATCH = 8
LINES = 48
COLS = 128
GROUP = 8
EPSILON = 1e-06
F32, BF16 = jnp.float32, jnp.bfloat16


def lanczos(x):
    return np.where(np.abs(x) < 4, np.sinc(x) * np.sinc(x / 4), 0.0)


def tap_table():
    taps = lanczos(np.arange(TAPS)[None, :] - 3 - np.arange(NBIN)[:, None] / NBIN)
    taps = taps.astype(np.float32).astype(ml_dtypes.bfloat16).astype(np.float32)
    return np.concatenate([np.zeros((1, TAPS), np.float32), taps]).reshape(-1)


def lobe_table():
    at = (np.arange(2 * OVERS) - OVERS) / OVERS
    lobes = lanczos(at[:, None] - (np.arange(PATCH) - (PATCH // 2 - 1))[None, :])
    return np.pad(lobes.astype(np.float32), ((0, 0), (0, 128 - PATCH)))


SIDES = [(i, j) for i in (-1, 0, 1) for j in (-1, 0, 1) if (i, j) != (0, 0)]


def exchange(axes, par, img, out_par, out, got_par, got, sems):
    lines, cols = img.shape[1:]
    here = [lax.axis_index(a) for a in axes]
    count = [lax.axis_size(a) for a in axes]

    def inside(i, j):
        row, col = here[0] + i, here[1] + j
        return (row >= 0) & (row < count[0]) & (col >= 0) & (col < count[1])

    got[...] = jnp.zeros_like(got)
    got_par[...] = jnp.zeros_like(got_par)
    barrier = pltpu.get_barrier_semaphore()
    for i, j in SIDES:

        @pl.when(inside(i, j))
        def _():
            pl.semaphore_signal(
                barrier,
                inc=1,
                device_id=(here[0] + i, here[1] + j),
                device_id_type=pl.DeviceIdType.MESH,
            )

    tall, wide = (
        1 + jnp.where(h > 0, 1, 0) + jnp.where(h < n - 1, 1, 0) for h, n in zip(here, count)
    )
    pl.semaphore_wait(barrier, tall * wide - 1)

    def spans(step, size, width):
        if step == 0:
            return pl.ds(0, size), pl.ds(width, size)
        if step == 1:
            return pl.ds(size - width, width), pl.ds(0, width)
        return pl.ds(0, width), pl.ds(width + size, width)

    def copies(k, i, j):
        src_l, dst_l = spans(i, lines, LINES)
        src_c, dst_c = spans(j, cols, COLS)
        where = dict(
            device_id=(here[0] + i, here[1] + j), device_id_type=pl.DeviceIdType.MESH
        )
        slot = 3 * (1 - i) + 1 - j
        return (
            pltpu.make_async_remote_copy(
                src_ref=img.at[:, src_l, src_c],
                dst_ref=got.at[:, dst_l, dst_c],
                send_sem=sems.at[0, k],
                recv_sem=sems.at[1, k],
                **where,
            ),
            pltpu.make_async_remote_copy(
                src_ref=par,
                dst_ref=got_par.at[slot],
                send_sem=sems.at[2, k],
                recv_sem=sems.at[3, k],
                **where,
            ),
        )

    for k, (i, j) in enumerate(SIDES):

        @pl.when(inside(i, j))
        def _():
            for copy in copies(k, i, j):
                copy.start()

    out[:, LINES : LINES + lines, COLS : COLS + cols] = img[...]
    out_par[4:5, :] = par[...]
    for k, (i, j) in enumerate(SIDES):

        @pl.when(inside(i, j))
        def _():
            for copy in copies(k, i, j):
                copy.wait_send()

        @pl.when(inside(-i, -j))
        def _():
            for copy in copies(k, i, j):
                copy.wait_recv()

    out[:, :LINES, :] = got[:, :LINES, :]
    out[:, LINES + lines :, :] = got[:, LINES + lines :, :]
    out[:, LINES : LINES + lines, :COLS] = got[:, LINES : LINES + lines, :COLS]
    out[:, LINES : LINES + lines, COLS + cols :] = got[:, LINES : LINES + lines, COLS + cols :]
    for slot in range(9):
        if slot != 4:
            out_par[slot : slot + 1, :] = got_par[slot]


def dot_nt(a, b, **kw):
    return lax.dot_general(a, b, (((1,), (1,)), ((), ())), preferred_element_type=F32, **kw)


def split3(x):
    hi = x.astype(BF16)
    rest = x - hi.astype(F32)
    mid = rest.astype(BF16)
    return hi, mid, (rest - mid.astype(F32)).astype(BF16)


def band(rows, span, base, tab, shift, f):
    gap = lax.broadcasted_iota(jnp.int32, (rows, span), 1) - lax.broadcasted_iota(
        jnp.int32, (rows, span), 0
    )
    gap = gap - (base - (TAPS // 2 - 1) + shift)
    out = jnp.zeros((rows, span), F32)
    for t in range(TAPS):
        out = jnp.where(gap == t, tab[f * TAPS + t], out)
    return out.astype(BF16)


def body(
    nu, nv, par, tab, mask, peaks, ext, ref, lobes, out, patch, amp, win, cen, wts, toep, tmp, tmp2,
    flat, flat2,
):
    chunks = (nv * CHIP + 2 * SEARCH + 127) // 128

    def fact(kind, u, v):
        side_u, side_v = u // nu, v // nv
        spot = (kind * nu + u - side_u * nu) * nv + v - side_v * nv
        return par[3 * (side_u + 1) + side_v + 1, spot]

    for u in range(-1, nu + 1):
        rows = CHIP if 0 <= u < nu else SEARCH
        first = u * CHIP + (CHIP - SEARCH if u < 0 else 0)
        low = (first + LINES - 12) // 16 * 16
        high = min(-(-(first + LINES + rows + 12) // 16) * 16, nu * CHIP + 2 * LINES)
        totals = [None] * chunks
        for v in range(-1, nv + 1):
            begin = max(v * CHIP, -SEARCH)
            end = min(v * CHIP + CHIP, nv * CHIP + SEARCH)
            left = (begin + COLS - 12) // 128 * 128
            right = left + 256
            a = band(rows, high - low, first + LINES - low, tab, fact(0, u, v), fact(2, u, v))
            half = jnp.concatenate(
                [
                    jnp.dot(a, ext[c, low:high, left:right], preferred_element_type=F32)
                    for c in range(2)
                ],
                axis=0,
            ).astype(BF16)
            b = band(
                end - begin, 256, begin + COLS - left, tab, fact(1, u, v), fact(3, u, v)
            )
            spot = begin + SEARCH
            while spot < end + SEARCH:
                m = spot // 128
                stop = min(end + SEARCH, (m + 1) * 128)
                part = b[spot - SEARCH - begin : stop - SEARCH - begin]
                pieces = [part]
                if spot > m * 128:
                    pieces.insert(0, jnp.zeros((spot - m * 128, 256), BF16))
                if stop < m * 128 + 128:
                    pieces.append(jnp.zeros((m * 128 + 128 - stop, 256), BF16))
                piece = jnp.concatenate(pieces, axis=0) if len(pieces) > 1 else part
                term = dot_nt(half, piece)
                totals[m] = term if totals[m] is None else totals[m] + term
                spot = stop
        for m in range(chunks):
            re, im = totals[m][:rows], totals[m][rows:]
            amp[first + SEARCH : first + SEARCH + rows, m * 128 : m * 128 + 128] = (
                jnp.sqrt(re * re + im * im).astype(BF16).astype(F32)
            )

    lane = lax.broadcasted_iota(jnp.int32, (2 * CHIP, 128), 1)
    low_lanes = lane < CHIP
    re = ref[0].astype(F32)
    im = ref[1].astype(F32)
    across = jnp.sqrt(re * re + im * im).astype(BF16).astype(F32).T
    for u in range(nu):
        for v in range(nv):
            n = u * nv + v
            lines = slice(u * CHIP, u * CHIP + 2 * CHIP)
            m = v // 2
            if v % 2 == 0:
                win[n] = amp[lines, m * 128 : m * 128 + 128]
            else:
                win[n] = jnp.where(
                    low_lanes,
                    pltpu.roll(amp[lines, m * 128 : m * 128 + 128], 64, 1),
                    pltpu.roll(amp[lines, m * 128 + 128 : m * 128 + 256], 64, 1),
                )
            wide = u // 2 * 128
            chip = across[v * CHIP : v * CHIP + CHIP, wide : wide + 128]
            if u % 2:
                chip = pltpu.roll(chip, 64, 1)
            keep = low_lanes[:CHIP]
            chip = jnp.where(keep, chip, 0.0)
            mean = jnp.sum(jnp.sum(chip, axis=1, keepdims=True), axis=0, keepdims=True)
            mean = mean * (1.0 / (CHIP * CHIP))
            cen[n] = jnp.where(keep, (chip - mean).astype(BF16).astype(F32), 0.0)

    gap_r = lax.broadcasted_iota(jnp.int32, (CHIP, 128), 1) - lax.broadcasted_iota(
        jnp.int32, (CHIP, 128), 0
    )
    ones_r = jnp.where((gap_r >= 0) & (gap_r < CHIP), 1.0, 0.0).astype(BF16)
    gap_c = lax.broadcasted_iota(jnp.int32, (128, 128), 0) - lane
    ones_c = jnp.where((gap_c >= 0) & (gap_c < CHIP), 1.0, 0.0).astype(BF16)

    def one_chip(n, carry):
        w = win[n]
        for s in range(GROUP):
            shifted = pltpu.roll(w, 128 - s, 1) if s else w
            wts[s * 128 : s * 128 + 128, :] = shifted.astype(BF16)
        centred = cen[n]
        for j in range(CHIP):
            k, s = j // GROUP, j % GROUP
            line = jnp.broadcast_to(centred[j : j + 1, :], (CHIP, 128))
            toep[k * CHIP : k * CHIP + CHIP, s * 128 : s * 128 + 128] = pltpu.roll(
                line, 0, 1, stride=1, stride_axis=0
            ).astype(BF16)
        prod = jnp.dot(toep[...], wts[...], preferred_element_type=F32)
        cross = prod[:CHIP]
        for k in range(1, CHIP // GROUP):
            cross = cross + pltpu.roll(prod[k * CHIP : k * CHIP + CHIP], 128 - k * GROUP, 1)
        energy = jnp.sum(jnp.sum(centred * centred, axis=1, keepdims=True), axis=0, keepdims=True)
        square = w * w
        square_hi = square.astype(BF16)
        square_lo = (square - square_hi.astype(F32)).astype(BF16)
        sums = jnp.dot(
            ones_r,
            jnp.concatenate([w.astype(BF16), square_hi, square_lo], axis=1),
            preferred_element_type=F32,
        )
        terms = split3(sums[:, :128]) + split3(sums[:, 128:256] + sums[:, 256:])
        boxes = jnp.dot(jnp.concatenate(terms, axis=0), ones_c, preferred_element_type=F32)
        box = [boxes[i * CHIP : i * CHIP + CHIP] for i in range(6)]
        total = box[2] + box[1] + box[0]
        squares = box[5] + box[4] + box[3]
        normed = cross / jnp.sqrt(
            energy * (squares - total * total * (1.0 / (CHIP * CHIP))) + EPSILON
        )
        land = (mask[n] == 1) & low_lanes[:CHIP]
        surface = jnp.where(land, normed, 0.0)
        tmp[...] = surface
        pairs = tmp[pl.ds(0, 32, stride=2), :] + pltpu.roll(tmp[pl.ds(1, 32, stride=2), :], 64, 1)
        flat[n] = pairs
        lead = SEARCH - (PATCH // 2 - 1)
        lobe_a = pltpu.roll(lobes[...], peaks[n] + lead, 1)
        lobe_d = pltpu.roll(lobes[...], peaks[nu * nv + n] + lead, 1)
        near = jnp.dot(
            lobe_a,
            jnp.concatenate([surface, jnp.zeros((CHIP, 128), F32)], axis=0),
            preferred_element_type=F32,
            precision=lax.Precision.HIGHEST,
        )
        tall = jnp.concatenate([lobe_d, jnp.zeros((96, 128), F32)], axis=0)
        tmp2[...] = dot_nt(near, tall, precision=lax.Precision.HIGHEST)
        quads = tmp2[pl.ds(0, 8, stride=4), :]
        for r in range(1, 4):
            quads = quads + pltpu.roll(tmp2[pl.ds(r, 8, stride=4), :], 32 * r, 1)
        flat2[n] = quads
        return carry

    lax.fori_loop(0, nu * nv, one_chip, 0)
    for u in range(nu):
        for v in range(nv):
            for m in range(CHIP // 2):
                out[u, v : v + 1, m * 128 : m * 128 + 128] = flat[u * nv + v, m : m + 1, :]
            for m in range(8):
                patch[u, v : v + 1, m * 128 : m * 128 + 128] = flat2[u * nv + v, m : m + 1, :]


def per_device(reference_image, secondary_image, block_shifts, shift_bins, land_mask, coarse_peaks):
    nu, nv = land_mask.shape
    par = jnp.concatenate([block_shifts, shift_bins + 1], axis=0).reshape(1, -1)
    par = jnp.pad(par, ((0, 0), (0, -par.shape[1] % 128)))
    smem = pl.BlockSpec(memory_space=pltpu.SMEM)
    vmem = pl.BlockSpec(memory_space=pltpu.VMEM)
    n = nu * nv
    chunks = (nv * CHIP + 2 * SEARCH + 127) // 128
    held = (2, nu * CHIP + 2 * LINES, nv * CHIP + 2 * COLS)

    def halo(*refs):
        exchange(("az", "rg"), *refs)

    par, ext = pl.pallas_call(
        halo,
        out_shape=(
            jax.ShapeDtypeStruct((9, par.shape[1]), jnp.int32),
            jax.ShapeDtypeStruct(held, BF16),
        ),
        in_specs=[vmem, vmem],
        out_specs=(vmem, vmem),
        scratch_shapes=[
            pltpu.VMEM((9, 1, par.shape[1]), jnp.int32),
            pltpu.VMEM(held, BF16),
            pltpu.SemaphoreType.DMA((4, 8)),
        ],
        compiler_params=pltpu.CompilerParams(
            collective_id=0, has_side_effects=True, vmem_limit_bytes=16 * 1024 * 1024
        ),
    )(par, secondary_image)

    def kernel(*refs):
        body(nu, nv, *refs)

    return pl.pallas_call(
        kernel,
        out_shape=(
            jax.ShapeDtypeStruct((nu, nv, CHIP * CHIP), F32),
            jax.ShapeDtypeStruct((nu, nv, 4 * OVERS * OVERS), F32),
        ),
        in_specs=[smem] * 4 + [vmem] * 3,
        out_specs=(vmem, vmem),
        scratch_shapes=[
            pltpu.VMEM((nu * CHIP + 2 * SEARCH, chunks * 128), F32),
            pltpu.VMEM((n, 2 * CHIP, 128), F32),
            pltpu.VMEM((n, CHIP, 128), F32),
            pltpu.VMEM((GROUP * 128, 128), BF16),
            pltpu.VMEM((CHIP * CHIP // GROUP, GROUP * 128), BF16),
            pltpu.VMEM((CHIP, 128), F32),
            pltpu.VMEM((2 * OVERS, 128), F32),
            pltpu.VMEM((n, CHIP // 2, 128), F32),
            pltpu.VMEM((n, 8, 128), F32),
        ],
        compiler_params=pltpu.CompilerParams(vmem_limit_bytes=48 * 1024 * 1024),
    )(
        par,
        jnp.asarray(tap_table()),
        land_mask.reshape(-1),
        coarse_peaks.reshape(-1),
        ext,
        reference_image,
        jnp.asarray(lobe_table()),
    )


def solution(mesh):
    cut = P(None, "az", "rg")
    return jax.shard_map(
        per_device,
        mesh=mesh,
        in_specs=(cut, cut, cut, cut, P("az", "rg"), cut),
        out_specs=(P("az", "rg", None), P("az", "rg", None)),
        check_vma=False,
    )
```

```python
import jax
import jax.numpy as jnp
import ml_dtypes
import numpy as np
from jax import lax
from jax.experimental import pallas as pl
from jax.experimental.pallas import tpu as pltpu
from jax.sharding import PartitionSpec as P

CHIP = 64
SEARCH = 32
TAPS = 8
NBIN = 16
OVERS = 16
PATCH = 8
LINES = 48
COLS = 128
GROUP = 8
EPSILON = 1e-06
F32, BF16 = jnp.float32, jnp.bfloat16


def lanczos(x):
    return np.where(np.abs(x) < 4, np.sinc(x) * np.sinc(x / 4), 0.0)


def tap_table():
    taps = lanczos(np.arange(TAPS)[None, :] - 3 - np.arange(NBIN)[:, None] / NBIN)
    taps = taps.astype(np.float32).astype(ml_dtypes.bfloat16).astype(np.float32)
    return np.concatenate([np.zeros((1, TAPS), np.float32), taps]).reshape(-1)


def lobe_table():
    at = (np.arange(2 * OVERS) - OVERS) / OVERS
    lobes = lanczos(at[:, None] - (np.arange(PATCH) - (PATCH // 2 - 1))[None, :])
    return np.pad(lobes.astype(np.float32), ((0, 0), (0, 128 - PATCH)))


SIDES = [(i, j) for i in (-1, 0, 1) for j in (-1, 0, 1) if (i, j) != (0, 0)]


def exchange(axes, shifts, bins, img, out_par, out, par, got_par, got, sems):
    lines, cols = img.shape[1:]
    here = [lax.axis_index(a) for a in axes]
    count = [lax.axis_size(a) for a in axes]

    def inside(i, j):
        row, col = here[0] + i, here[1] + j
        return (row >= 0) & (row < count[0]) & (col >= 0) & (col < count[1])

    rows = [shifts[k, u : u + 1, :] for k in range(2) for u in range(shifts.shape[1])]
    rows += [bins[k, u : u + 1, :] + 1 for k in range(2) for u in range(shifts.shape[1])]
    rest = par.shape[1] - len(rows) * shifts.shape[2]
    if rest:
        rows.append(jnp.zeros((1, rest), jnp.int32))
    par[...] = jnp.concatenate(rows, axis=1)
    got[...] = jnp.zeros_like(got)
    got_par[...] = jnp.zeros_like(got_par)
    barrier = pltpu.get_barrier_semaphore()
    for i, j in SIDES:

        @pl.when(inside(i, j))
        def _():
            pl.semaphore_signal(
                barrier,
                inc=1,
                device_id=(here[0] + i, here[1] + j),
                device_id_type=pl.DeviceIdType.MESH,
            )

    tall, wide = (
        1 + jnp.where(h > 0, 1, 0) + jnp.where(h < n - 1, 1, 0) for h, n in zip(here, count)
    )
    pl.semaphore_wait(barrier, tall * wide - 1)

    def spans(step, size, width):
        if step == 0:
            return pl.ds(0, size), pl.ds(width, size)
        if step == 1:
            return pl.ds(size - width, width), pl.ds(0, width)
        return pl.ds(0, width), pl.ds(width + size, width)

    def copies(k, i, j):
        src_l, dst_l = spans(i, lines, LINES)
        src_c, dst_c = spans(j, cols, COLS)
        where = dict(
            device_id=(here[0] + i, here[1] + j), device_id_type=pl.DeviceIdType.MESH
        )
        slot = 3 * (1 - i) + 1 - j
        return (
            pltpu.make_async_remote_copy(
                src_ref=img.at[:, src_l, src_c],
                dst_ref=got.at[:, dst_l, dst_c],
                send_sem=sems.at[0, k],
                recv_sem=sems.at[1, k],
                **where,
            ),
            pltpu.make_async_remote_copy(
                src_ref=par,
                dst_ref=got_par.at[slot],
                send_sem=sems.at[2, k],
                recv_sem=sems.at[3, k],
                **where,
            ),
        )

    for k, (i, j) in enumerate(SIDES):

        @pl.when(inside(i, j))
        def _():
            for copy in copies(k, i, j):
                copy.start()

    out[:, LINES : LINES + lines, COLS : COLS + cols] = img[...]
    out_par[4:5, :] = par[...]
    for k, (i, j) in enumerate(SIDES):

        @pl.when(inside(i, j))
        def _():
            for copy in copies(k, i, j):
                copy.wait_send()

        @pl.when(inside(-i, -j))
        def _():
            for copy in copies(k, i, j):
                copy.wait_recv()

    out[:, :LINES, :] = got[:, :LINES, :]
    out[:, LINES + lines :, :] = got[:, LINES + lines :, :]
    out[:, LINES : LINES + lines, :COLS] = got[:, LINES : LINES + lines, :COLS]
    out[:, LINES : LINES + lines, COLS + cols :] = got[:, LINES : LINES + lines, COLS + cols :]
    for slot in range(9):
        if slot != 4:
            out_par[slot : slot + 1, :] = got_par[slot]


def dot_nt(a, b, **kw):
    return lax.dot_general(a, b, (((1,), (1,)), ((), ())), preferred_element_type=F32, **kw)


def split3(x):
    hi = x.astype(BF16)
    rest = x - hi.astype(F32)
    mid = rest.astype(BF16)
    return hi, mid, (rest - mid.astype(F32)).astype(BF16)


def band(rows, span, base, tab, shift, f):
    gap = lax.broadcasted_iota(jnp.int32, (rows, span), 1) - lax.broadcasted_iota(
        jnp.int32, (rows, span), 0
    )
    gap = gap - (base - (TAPS // 2 - 1) + shift)
    out = jnp.zeros((rows, span), F32)
    for t in range(TAPS):
        out = jnp.where(gap == t, tab[f * TAPS + t], out)
    return out.astype(BF16)


def body(
    nu, nv, par, tab, mask, peaks, ext, ref, lobes, out, patch, amp, win, cen, wts, toep, tmp, tmp2,
    flat, flat2,
):
    chunks = (nv * CHIP + 2 * SEARCH + 127) // 128

    def fact(kind, u, v):
        side_u, side_v = u // nu, v // nv
        spot = (kind * nu + u - side_u * nu) * nv + v - side_v * nv
        return par[3 * (side_u + 1) + side_v + 1, spot]

    for u in range(-1, nu + 1):
        rows = CHIP if 0 <= u < nu else SEARCH
        first = u * CHIP + (CHIP - SEARCH if u < 0 else 0)
        low = (first + LINES - 12) // 16 * 16
        high = min(-(-(first + LINES + rows + 12) // 16) * 16, nu * CHIP + 2 * LINES)
        totals = [None] * chunks
        for v in range(-1, nv + 1):
            begin = max(v * CHIP, -SEARCH)
            end = min(v * CHIP + CHIP, nv * CHIP + SEARCH)
            left = (begin + COLS - 12) // 128 * 128
            right = left + 256
            a = band(rows, high - low, first + LINES - low, tab, fact(0, u, v), fact(2, u, v))
            half = jnp.concatenate(
                [
                    jnp.dot(a, ext[c, low:high, left:right], preferred_element_type=F32)
                    for c in range(2)
                ],
                axis=0,
            ).astype(BF16)
            b = band(
                end - begin, 256, begin + COLS - left, tab, fact(1, u, v), fact(3, u, v)
            )
            spot = begin + SEARCH
            while spot < end + SEARCH:
                m = spot // 128
                stop = min(end + SEARCH, (m + 1) * 128)
                part = b[spot - SEARCH - begin : stop - SEARCH - begin]
                pieces = [part]
                if spot > m * 128:
                    pieces.insert(0, jnp.zeros((spot - m * 128, 256), BF16))
                if stop < m * 128 + 128:
                    pieces.append(jnp.zeros((m * 128 + 128 - stop, 256), BF16))
                piece = jnp.concatenate(pieces, axis=0) if len(pieces) > 1 else part
                term = dot_nt(half, piece)
                totals[m] = term if totals[m] is None else totals[m] + term
                spot = stop
        for m in range(chunks):
            re, im = totals[m][:rows], totals[m][rows:]
            amp[first + SEARCH : first + SEARCH + rows, m * 128 : m * 128 + 128] = (
                jnp.sqrt(re * re + im * im).astype(BF16).astype(F32)
            )

    lane = lax.broadcasted_iota(jnp.int32, (2 * CHIP, 128), 1)
    low_lanes = lane < CHIP
    re = ref[0].astype(F32)
    im = ref[1].astype(F32)
    across = jnp.sqrt(re * re + im * im).astype(BF16).astype(F32).T
    for u in range(nu):
        for v in range(nv):
            n = u * nv + v
            lines = slice(u * CHIP, u * CHIP + 2 * CHIP)
            m = v // 2
            if v % 2 == 0:
                win[n] = amp[lines, m * 128 : m * 128 + 128]
            else:
                win[n] = jnp.where(
                    low_lanes,
                    pltpu.roll(amp[lines, m * 128 : m * 128 + 128], 64, 1),
                    pltpu.roll(amp[lines, m * 128 + 128 : m * 128 + 256], 64, 1),
                )
            wide = u // 2 * 128
            chip = across[v * CHIP : v * CHIP + CHIP, wide : wide + 128]
            if u % 2:
                chip = pltpu.roll(chip, 64, 1)
            keep = low_lanes[:CHIP]
            chip = jnp.where(keep, chip, 0.0)
            mean = jnp.sum(jnp.sum(chip, axis=1, keepdims=True), axis=0, keepdims=True)
            mean = mean * (1.0 / (CHIP * CHIP))
            cen[n] = jnp.where(keep, (chip - mean).astype(BF16).astype(F32), 0.0)

    gap_r = lax.broadcasted_iota(jnp.int32, (CHIP, 128), 1) - lax.broadcasted_iota(
        jnp.int32, (CHIP, 128), 0
    )
    ones_r = jnp.where((gap_r >= 0) & (gap_r < CHIP), 1.0, 0.0).astype(BF16)
    gap_c = lax.broadcasted_iota(jnp.int32, (128, 128), 0) - lane
    ones_c = jnp.where((gap_c >= 0) & (gap_c < CHIP), 1.0, 0.0).astype(BF16)

    def one_chip(n, carry):
        w = win[n]
        for s in range(GROUP):
            shifted = pltpu.roll(w, 128 - s, 1) if s else w
            wts[s * 128 : s * 128 + 128, :] = shifted.astype(BF16)
        centred = cen[n]
        for j in range(CHIP):
            k, s = j // GROUP, j % GROUP
            line = jnp.broadcast_to(centred[j : j + 1, :], (CHIP, 128))
            toep[k * CHIP : k * CHIP + CHIP, s * 128 : s * 128 + 128] = pltpu.roll(
                line, 0, 1, stride=1, stride_axis=0
            ).astype(BF16)
        prod = jnp.dot(toep[...], wts[...], preferred_element_type=F32)
        cross = prod[:CHIP]
        for k in range(1, CHIP // GROUP):
            cross = cross + pltpu.roll(prod[k * CHIP : k * CHIP + CHIP], 128 - k * GROUP, 1)
        energy = jnp.sum(jnp.sum(centred * centred, axis=1, keepdims=True), axis=0, keepdims=True)
        square = w * w
        square_hi = square.astype(BF16)
        square_lo = (square - square_hi.astype(F32)).astype(BF16)
        sums = jnp.dot(
            ones_r,
            jnp.concatenate([w.astype(BF16), square_hi, square_lo], axis=1),
            preferred_element_type=F32,
        )
        terms = split3(sums[:, :128]) + split3(sums[:, 128:256] + sums[:, 256:])
        boxes = jnp.dot(jnp.concatenate(terms, axis=0), ones_c, preferred_element_type=F32)
        box = [boxes[i * CHIP : i * CHIP + CHIP] for i in range(6)]
        total = box[2] + box[1] + box[0]
        squares = box[5] + box[4] + box[3]
        normed = cross / jnp.sqrt(
            energy * (squares - total * total * (1.0 / (CHIP * CHIP))) + EPSILON
        )
        land = (mask[n // nv, n % nv] == 1) & low_lanes[:CHIP]
        surface = jnp.where(land, normed, 0.0)
        tmp[...] = surface
        pairs = tmp[pl.ds(0, 32, stride=2), :] + pltpu.roll(tmp[pl.ds(1, 32, stride=2), :], 64, 1)
        flat[n] = pairs
        lead = SEARCH - (PATCH // 2 - 1)
        lobe_a = pltpu.roll(lobes[...], peaks[0, n // nv, n % nv] + lead, 1)
        lobe_d = pltpu.roll(lobes[...], peaks[1, n // nv, n % nv] + lead, 1)
        near = jnp.dot(
            lobe_a,
            jnp.concatenate([surface, jnp.zeros((CHIP, 128), F32)], axis=0),
            preferred_element_type=F32,
            precision=lax.Precision.HIGHEST,
        )
        tall = jnp.concatenate([lobe_d, jnp.zeros((96, 128), F32)], axis=0)
        tmp2[...] = dot_nt(near, tall, precision=lax.Precision.HIGHEST)
        quads = tmp2[pl.ds(0, 8, stride=4), :]
        for r in range(1, 4):
            quads = quads + pltpu.roll(tmp2[pl.ds(r, 8, stride=4), :], 32 * r, 1)
        flat2[n] = quads
        return carry

    lax.fori_loop(0, nu * nv, one_chip, 0)
    for u in range(nu):
        for v in range(nv):
            for m in range(CHIP // 2):
                out[u, v : v + 1, m * 128 : m * 128 + 128] = flat[u * nv + v, m : m + 1, :]
            for m in range(8):
                patch[u, v : v + 1, m * 128 : m * 128 + 128] = flat2[u * nv + v, m : m + 1, :]


def per_device(reference_image, secondary_image, block_shifts, shift_bins, land_mask, coarse_peaks):
    nu, nv = land_mask.shape
    facts = -(-4 * nu * nv // 128) * 128
    smem = pl.BlockSpec(memory_space=pltpu.SMEM)
    vmem = pl.BlockSpec(memory_space=pltpu.VMEM)
    n = nu * nv
    chunks = (nv * CHIP + 2 * SEARCH + 127) // 128
    held = (2, nu * CHIP + 2 * LINES, nv * CHIP + 2 * COLS)

    def halo(*refs):
        exchange(("az", "rg"), *refs)

    par, ext = pl.pallas_call(
        halo,
        out_shape=(
            jax.ShapeDtypeStruct((9, facts), jnp.int32),
            jax.ShapeDtypeStruct(held, BF16),
        ),
        in_specs=[vmem, vmem, vmem],
        out_specs=(vmem, vmem),
        scratch_shapes=[
            pltpu.VMEM((1, facts), jnp.int32),
            pltpu.VMEM((9, 1, facts), jnp.int32),
            pltpu.VMEM(held, BF16),
            pltpu.SemaphoreType.DMA((4, 8)),
        ],
        compiler_params=pltpu.CompilerParams(
            collective_id=0, has_side_effects=True, vmem_limit_bytes=16 * 1024 * 1024
        ),
    )(block_shifts, shift_bins, secondary_image)

    def kernel(*refs):
        body(nu, nv, *refs)

    return pl.pallas_call(
        kernel,
        out_shape=(
            jax.ShapeDtypeStruct((nu, nv, CHIP * CHIP), F32),
            jax.ShapeDtypeStruct((nu, nv, 4 * OVERS * OVERS), F32),
        ),
        in_specs=[smem] * 4 + [vmem] * 3,
        out_specs=(vmem, vmem),
        scratch_shapes=[
            pltpu.VMEM((nu * CHIP + 2 * SEARCH, chunks * 128), F32),
            pltpu.VMEM((n, 2 * CHIP, 128), F32),
            pltpu.VMEM((n, CHIP, 128), F32),
            pltpu.VMEM((GROUP * 128, 128), BF16),
            pltpu.VMEM((CHIP * CHIP // GROUP, GROUP * 128), BF16),
            pltpu.VMEM((CHIP, 128), F32),
            pltpu.VMEM((2 * OVERS, 128), F32),
            pltpu.VMEM((n, CHIP // 2, 128), F32),
            pltpu.VMEM((n, 8, 128), F32),
        ],
        compiler_params=pltpu.CompilerParams(vmem_limit_bytes=48 * 1024 * 1024),
    )(
        par,
        jnp.asarray(tap_table()),
        land_mask,
        coarse_peaks,
        ext,
        reference_image,
        jnp.asarray(lobe_table()),
    )


def solution(mesh):
    cut = P(None, "az", "rg")
    return jax.shard_map(
        per_device,
        mesh=mesh,
        in_specs=(cut, cut, cut, cut, P("az", "rg"), cut),
        out_specs=(P("az", "rg", None), P("az", "rg", None)),
        check_vma=False,
    )
```

```python
import jax
import jax.numpy as jnp
import ml_dtypes
import numpy as np
from jax import lax
from jax.experimental import pallas as pl
from jax.experimental.pallas import tpu as pltpu
from jax.sharding import PartitionSpec as P

CHIP = 64
SEARCH = 32
TAPS = 8
NBIN = 16
OVERS = 16
PATCH = 8
LINES = 48
COLS = 128
GROUP = 8
EPSILON = 1e-06
F32, BF16 = jnp.float32, jnp.bfloat16


def lanczos(x):
    return np.where(np.abs(x) < 4, np.sinc(x) * np.sinc(x / 4), 0.0)


def tap_table():
    taps = lanczos(np.arange(TAPS)[None, :] - 3 - np.arange(NBIN)[:, None] / NBIN)
    taps = taps.astype(np.float32).astype(ml_dtypes.bfloat16).astype(np.float32)
    return np.concatenate([np.zeros((1, TAPS), np.float32), taps]).reshape(-1)


def lobe_table():
    at = (np.arange(2 * OVERS) - OVERS) / OVERS
    lobes = lanczos(at[:, None] - (np.arange(PATCH) - (PATCH // 2 - 1))[None, :])
    return np.pad(lobes.astype(np.float32), ((0, 0), (0, 128 - PATCH)))


SIDES = [(i, j) for i in (-1, 0, 1) for j in (-1, 0, 1) if (i, j) != (0, 0)]


def exchange(
    axes, far_shifts, far_bins, far_img, out_par, out, shifts, bins, img, near_sems, par, got_par, got, sems
):
    lines, cols = img.shape[1:]
    here = [lax.axis_index(a) for a in axes]
    count = [lax.axis_size(a) for a in axes]

    def inside(i, j):
        row, col = here[0] + i, here[1] + j
        return (row >= 0) & (row < count[0]) & (col >= 0) & (col < count[1])

    loads = [
        pltpu.make_async_copy(far, near, near_sems.at[k])
        for k, (far, near) in enumerate(
            ((far_img, img), (far_shifts, shifts), (far_bins, bins))
        )
    ]
    for load in loads:
        load.start()
    got[...] = jnp.zeros_like(got)
    got_par[...] = jnp.zeros_like(got_par)
    barrier = pltpu.get_barrier_semaphore()
    for i, j in SIDES:

        @pl.when(inside(i, j))
        def _():
            pl.semaphore_signal(
                barrier,
                inc=1,
                device_id=(here[0] + i, here[1] + j),
                device_id_type=pl.DeviceIdType.MESH,
            )

    tall, wide = (
        1 + jnp.where(h > 0, 1, 0) + jnp.where(h < n - 1, 1, 0) for h, n in zip(here, count)
    )
    for load in loads:
        load.wait()
    rows = [shifts[k, u : u + 1, :] for k in range(2) for u in range(shifts.shape[1])]
    rows += [bins[k, u : u + 1, :] + 1 for k in range(2) for u in range(shifts.shape[1])]
    rest = par.shape[1] - len(rows) * shifts.shape[2]
    if rest:
        rows.append(jnp.zeros((1, rest), jnp.int32))
    par[...] = jnp.concatenate(rows, axis=1)
    pl.semaphore_wait(barrier, tall * wide - 1)

    def spans(step, size, width):
        if step == 0:
            return pl.ds(0, size), pl.ds(width, size)
        if step == 1:
            return pl.ds(size - width, width), pl.ds(0, width)
        return pl.ds(0, width), pl.ds(width + size, width)

    def copies(k, i, j):
        src_l, dst_l = spans(i, lines, LINES)
        src_c, dst_c = spans(j, cols, COLS)
        where = dict(
            device_id=(here[0] + i, here[1] + j), device_id_type=pl.DeviceIdType.MESH
        )
        slot = 3 * (1 - i) + 1 - j
        return (
            pltpu.make_async_remote_copy(
                src_ref=img.at[:, src_l, src_c],
                dst_ref=got.at[:, dst_l, dst_c],
                send_sem=sems.at[0, k],
                recv_sem=sems.at[1, k],
                **where,
            ),
            pltpu.make_async_remote_copy(
                src_ref=par,
                dst_ref=got_par.at[slot],
                send_sem=sems.at[2, k],
                recv_sem=sems.at[3, k],
                **where,
            ),
        )

    for k, (i, j) in enumerate(SIDES):

        @pl.when(inside(i, j))
        def _():
            for copy in copies(k, i, j):
                copy.start()

    out[:, LINES : LINES + lines, COLS : COLS + cols] = img[...]
    out_par[4:5, :] = par[...]
    for k, (i, j) in enumerate(SIDES):

        @pl.when(inside(i, j))
        def _():
            for copy in copies(k, i, j):
                copy.wait_send()

        @pl.when(inside(-i, -j))
        def _():
            for copy in copies(k, i, j):
                copy.wait_recv()

    out[:, :LINES, :] = got[:, :LINES, :]
    out[:, LINES + lines :, :] = got[:, LINES + lines :, :]
    out[:, LINES : LINES + lines, :COLS] = got[:, LINES : LINES + lines, :COLS]
    out[:, LINES : LINES + lines, COLS + cols :] = got[:, LINES : LINES + lines, COLS + cols :]
    for slot in range(9):
        if slot != 4:
            out_par[slot : slot + 1, :] = got_par[slot]


def dot_nt(a, b, **kw):
    return lax.dot_general(a, b, (((1,), (1,)), ((), ())), preferred_element_type=F32, **kw)


def split3(x):
    hi = x.astype(BF16)
    rest = x - hi.astype(F32)
    mid = rest.astype(BF16)
    return hi, mid, (rest - mid.astype(F32)).astype(BF16)


def band(rows, span, base, tab, shift, f):
    gap = lax.broadcasted_iota(jnp.int32, (rows, span), 1) - lax.broadcasted_iota(
        jnp.int32, (rows, span), 0
    )
    gap = gap - (base - (TAPS // 2 - 1) + shift)
    out = jnp.zeros((rows, span), F32)
    for t in range(TAPS):
        out = jnp.where(gap == t, tab[f * TAPS + t], out)
    return out.astype(BF16)


def body(
    nu, nv, par, tab, mask, peaks, ext, ref, lobes, out, patch, amp, win, cen, wts, toep, tmp, tmp2,
    flat, flat2,
):
    chunks = (nv * CHIP + 2 * SEARCH + 127) // 128

    def fact(kind, u, v):
        side_u, side_v = u // nu, v // nv
        spot = (kind * nu + u - side_u * nu) * nv + v - side_v * nv
        return par[3 * (side_u + 1) + side_v + 1, spot]

    for u in range(-1, nu + 1):
        rows = CHIP if 0 <= u < nu else SEARCH
        first = u * CHIP + (CHIP - SEARCH if u < 0 else 0)
        low = (first + LINES - 12) // 16 * 16
        high = min(-(-(first + LINES + rows + 12) // 16) * 16, nu * CHIP + 2 * LINES)
        totals = [None] * chunks
        for v in range(-1, nv + 1):
            begin = max(v * CHIP, -SEARCH)
            end = min(v * CHIP + CHIP, nv * CHIP + SEARCH)
            left = (begin + COLS - 12) // 128 * 128
            right = left + 256
            a = band(rows, high - low, first + LINES - low, tab, fact(0, u, v), fact(2, u, v))
            half = jnp.concatenate(
                [
                    jnp.dot(a, ext[c, low:high, left:right], preferred_element_type=F32)
                    for c in range(2)
                ],
                axis=0,
            ).astype(BF16)
            b = band(
                end - begin, 256, begin + COLS - left, tab, fact(1, u, v), fact(3, u, v)
            )
            spot = begin + SEARCH
            while spot < end + SEARCH:
                m = spot // 128
                stop = min(end + SEARCH, (m + 1) * 128)
                part = b[spot - SEARCH - begin : stop - SEARCH - begin]
                pieces = [part]
                if spot > m * 128:
                    pieces.insert(0, jnp.zeros((spot - m * 128, 256), BF16))
                if stop < m * 128 + 128:
                    pieces.append(jnp.zeros((m * 128 + 128 - stop, 256), BF16))
                piece = jnp.concatenate(pieces, axis=0) if len(pieces) > 1 else part
                term = dot_nt(half, piece)
                totals[m] = term if totals[m] is None else totals[m] + term
                spot = stop
        for m in range(chunks):
            re, im = totals[m][:rows], totals[m][rows:]
            amp[first + SEARCH : first + SEARCH + rows, m * 128 : m * 128 + 128] = (
                jnp.sqrt(re * re + im * im).astype(BF16).astype(F32)
            )

    lane = lax.broadcasted_iota(jnp.int32, (2 * CHIP, 128), 1)
    low_lanes = lane < CHIP
    re = ref[0].astype(F32)
    im = ref[1].astype(F32)
    across = jnp.sqrt(re * re + im * im).astype(BF16).astype(F32).T
    for u in range(nu):
        for v in range(nv):
            n = u * nv + v
            lines = slice(u * CHIP, u * CHIP + 2 * CHIP)
            m = v // 2
            if v % 2 == 0:
                win[n] = amp[lines, m * 128 : m * 128 + 128]
            else:
                win[n] = jnp.where(
                    low_lanes,
                    pltpu.roll(amp[lines, m * 128 : m * 128 + 128], 64, 1),
                    pltpu.roll(amp[lines, m * 128 + 128 : m * 128 + 256], 64, 1),
                )
            wide = u // 2 * 128
            chip = across[v * CHIP : v * CHIP + CHIP, wide : wide + 128]
            if u % 2:
                chip = pltpu.roll(chip, 64, 1)
            keep = low_lanes[:CHIP]
            chip = jnp.where(keep, chip, 0.0)
            mean = jnp.sum(jnp.sum(chip, axis=1, keepdims=True), axis=0, keepdims=True)
            mean = mean * (1.0 / (CHIP * CHIP))
            cen[n] = jnp.where(keep, (chip - mean).astype(BF16).astype(F32), 0.0)

    gap_r = lax.broadcasted_iota(jnp.int32, (CHIP, 128), 1) - lax.broadcasted_iota(
        jnp.int32, (CHIP, 128), 0
    )
    ones_r = jnp.where((gap_r >= 0) & (gap_r < CHIP), 1.0, 0.0).astype(BF16)
    gap_c = lax.broadcasted_iota(jnp.int32, (128, 128), 0) - lane
    ones_c = jnp.where((gap_c >= 0) & (gap_c < CHIP), 1.0, 0.0).astype(BF16)

    def one_chip(n, carry):
        w = win[n]
        for s in range(GROUP):
            shifted = pltpu.roll(w, 128 - s, 1) if s else w
            wts[s * 128 : s * 128 + 128, :] = shifted.astype(BF16)
        centred = cen[n]
        for j in range(CHIP):
            k, s = j // GROUP, j % GROUP
            line = jnp.broadcast_to(centred[j : j + 1, :], (CHIP, 128))
            toep[k * CHIP : k * CHIP + CHIP, s * 128 : s * 128 + 128] = pltpu.roll(
                line, 0, 1, stride=1, stride_axis=0
            ).astype(BF16)
        prod = jnp.dot(toep[...], wts[...], preferred_element_type=F32)
        cross = prod[:CHIP]
        for k in range(1, CHIP // GROUP):
            cross = cross + pltpu.roll(prod[k * CHIP : k * CHIP + CHIP], 128 - k * GROUP, 1)
        energy = jnp.sum(jnp.sum(centred * centred, axis=1, keepdims=True), axis=0, keepdims=True)
        square = w * w
        square_hi = square.astype(BF16)
        square_lo = (square - square_hi.astype(F32)).astype(BF16)
        sums = jnp.dot(
            ones_r,
            jnp.concatenate([w.astype(BF16), square_hi, square_lo], axis=1),
            preferred_element_type=F32,
        )
        terms = split3(sums[:, :128]) + split3(sums[:, 128:256] + sums[:, 256:])
        boxes = jnp.dot(jnp.concatenate(terms, axis=0), ones_c, preferred_element_type=F32)
        box = [boxes[i * CHIP : i * CHIP + CHIP] for i in range(6)]
        total = box[2] + box[1] + box[0]
        squares = box[5] + box[4] + box[3]
        normed = cross / jnp.sqrt(
            energy * (squares - total * total * (1.0 / (CHIP * CHIP))) + EPSILON
        )
        land = (mask[n // nv, n % nv] == 1) & low_lanes[:CHIP]
        surface = jnp.where(land, normed, 0.0)
        tmp[...] = surface
        pairs = tmp[pl.ds(0, 32, stride=2), :] + pltpu.roll(tmp[pl.ds(1, 32, stride=2), :], 64, 1)
        flat[n] = pairs
        lead = SEARCH - (PATCH // 2 - 1)
        lobe_a = pltpu.roll(lobes[...], peaks[0, n // nv, n % nv] + lead, 1)
        lobe_d = pltpu.roll(lobes[...], peaks[1, n // nv, n % nv] + lead, 1)
        near = jnp.dot(
            lobe_a,
            jnp.concatenate([surface, jnp.zeros((CHIP, 128), F32)], axis=0),
            preferred_element_type=F32,
            precision=lax.Precision.HIGHEST,
        )
        tall = jnp.concatenate([lobe_d, jnp.zeros((96, 128), F32)], axis=0)
        tmp2[...] = dot_nt(near, tall, precision=lax.Precision.HIGHEST)
        quads = tmp2[pl.ds(0, 8, stride=4), :]
        for r in range(1, 4):
            quads = quads + pltpu.roll(tmp2[pl.ds(r, 8, stride=4), :], 32 * r, 1)
        flat2[n] = quads
        return carry

    lax.fori_loop(0, nu * nv, one_chip, 0)
    for u in range(nu):
        for v in range(nv):
            for m in range(CHIP // 2):
                out[u, v : v + 1, m * 128 : m * 128 + 128] = flat[u * nv + v, m : m + 1, :]
            for m in range(8):
                patch[u, v : v + 1, m * 128 : m * 128 + 128] = flat2[u * nv + v, m : m + 1, :]


def per_device(reference_image, secondary_image, block_shifts, shift_bins, land_mask, coarse_peaks):
    nu, nv = land_mask.shape
    facts = -(-4 * nu * nv // 128) * 128
    smem = pl.BlockSpec(memory_space=pltpu.SMEM)
    vmem = pl.BlockSpec(memory_space=pltpu.VMEM)
    n = nu * nv
    chunks = (nv * CHIP + 2 * SEARCH + 127) // 128
    held = (2, nu * CHIP + 2 * LINES, nv * CHIP + 2 * COLS)

    def halo(*refs):
        exchange(("az", "rg"), *refs)

    par, ext = pl.pallas_call(
        halo,
        out_shape=(
            jax.ShapeDtypeStruct((9, facts), jnp.int32),
            jax.ShapeDtypeStruct(held, BF16),
        ),
        in_specs=[pl.BlockSpec(memory_space=pltpu.HBM)] * 3,
        out_specs=(vmem, vmem),
        scratch_shapes=[
            pltpu.VMEM(block_shifts.shape, jnp.int32),
            pltpu.VMEM(shift_bins.shape, jnp.int32),
            pltpu.VMEM(secondary_image.shape, BF16),
            pltpu.SemaphoreType.DMA((3,)),
            pltpu.VMEM((1, facts), jnp.int32),
            pltpu.VMEM((9, 1, facts), jnp.int32),
            pltpu.VMEM(held, BF16),
            pltpu.SemaphoreType.DMA((4, 8)),
        ],
        compiler_params=pltpu.CompilerParams(
            collective_id=0, has_side_effects=True, vmem_limit_bytes=63 * 1024 * 1024
        ),
    )(block_shifts, shift_bins, secondary_image)

    def kernel(*refs):
        body(nu, nv, *refs)

    return pl.pallas_call(
        kernel,
        out_shape=(
            jax.ShapeDtypeStruct((nu, nv, CHIP * CHIP), F32),
            jax.ShapeDtypeStruct((nu, nv, 4 * OVERS * OVERS), F32),
        ),
        in_specs=[smem] * 4 + [vmem] * 3,
        out_specs=(vmem, vmem),
        scratch_shapes=[
            pltpu.VMEM((nu * CHIP + 2 * SEARCH, chunks * 128), F32),
            pltpu.VMEM((n, 2 * CHIP, 128), F32),
            pltpu.VMEM((n, CHIP, 128), F32),
            pltpu.VMEM((GROUP * 128, 128), BF16),
            pltpu.VMEM((CHIP * CHIP // GROUP, GROUP * 128), BF16),
            pltpu.VMEM((CHIP, 128), F32),
            pltpu.VMEM((2 * OVERS, 128), F32),
            pltpu.VMEM((n, CHIP // 2, 128), F32),
            pltpu.VMEM((n, 8, 128), F32),
        ],
        compiler_params=pltpu.CompilerParams(vmem_limit_bytes=63 * 1024 * 1024),
    )(
        par,
        jnp.asarray(tap_table()),
        land_mask,
        coarse_peaks,
        ext,
        reference_image,
        jnp.asarray(lobe_table()),
    )


def solution(mesh):
    cut = P(None, "az", "rg")
    return jax.shard_map(
        per_device,
        mesh=mesh,
        in_specs=(cut, cut, cut, cut, P("az", "rg"), cut),
        out_specs=(P("az", "rg", None), P("az", "rg", None)),
        check_vma=False,
    )
```

```python
import jax
import jax.numpy as jnp
import ml_dtypes
import numpy as np
from jax import lax
from jax.experimental import pallas as pl
from jax.experimental.pallas import tpu as pltpu
from jax.sharding import PartitionSpec as P

CHIP = 64
SEARCH = 32
TAPS = 8
NBIN = 16
OVERS = 16
PATCH = 8
LINES = 48
COLS = 128
GROUP = 8
EPSILON = 1e-06
F32, BF16 = jnp.float32, jnp.bfloat16


def lanczos(x):
    return np.where(np.abs(x) < 4, np.sinc(x) * np.sinc(x / 4), 0.0)


def tap_table():
    taps = lanczos(np.arange(TAPS)[None, :] - 3 - np.arange(NBIN)[:, None] / NBIN)
    taps = taps.astype(np.float32).astype(ml_dtypes.bfloat16).astype(np.float32)
    return np.concatenate([np.zeros((1, TAPS), np.float32), taps]).reshape(-1)


def lobe_table():
    at = (np.arange(2 * OVERS) - OVERS) / OVERS
    lobes = lanczos(at[:, None] - (np.arange(PATCH) - (PATCH // 2 - 1))[None, :])
    return np.pad(lobes.astype(np.float32), ((0, 0), (0, 128 - PATCH)))


SIDES = [(i, j) for i in (-1, 0, 1) for j in (-1, 0, 1) if (i, j) != (0, 0)]


def exchange(
    axes, far_shifts, far_bins, far_img, out_par, out, shifts, bins, img, near_sems, par, got_par, got, sems
):
    lines, cols = img.shape[1:]
    here = [lax.axis_index(a) for a in axes]
    count = [lax.axis_size(a) for a in axes]

    def inside(i, j):
        row, col = here[0] + i, here[1] + j
        return (row >= 0) & (row < count[0]) & (col >= 0) & (col < count[1])

    loads = [
        pltpu.make_async_copy(far, near, near_sems.at[k])
        for k, (far, near) in enumerate(
            ((far_img, img), (far_shifts, shifts), (far_bins, bins))
        )
    ]
    for load in loads:
        load.start()
    got[...] = jnp.zeros_like(got)
    got_par[...] = jnp.zeros_like(got_par)
    barrier = pltpu.get_barrier_semaphore()
    for i, j in SIDES:

        @pl.when(inside(i, j))
        def _():
            pl.semaphore_signal(
                barrier,
                inc=1,
                device_id=(here[0] + i, here[1] + j),
                device_id_type=pl.DeviceIdType.MESH,
            )

    tall, wide = (
        1 + jnp.where(h > 0, 1, 0) + jnp.where(h < n - 1, 1, 0) for h, n in zip(here, count)
    )
    for load in loads:
        load.wait()
    rows = [shifts[k, u : u + 1, :] for k in range(2) for u in range(shifts.shape[1])]
    rows += [bins[k, u : u + 1, :] + 1 for k in range(2) for u in range(shifts.shape[1])]
    rest = par.shape[1] - len(rows) * shifts.shape[2]
    if rest:
        rows.append(jnp.zeros((1, rest), jnp.int32))
    par[...] = jnp.concatenate(rows, axis=1)
    pl.semaphore_wait(barrier, tall * wide - 1)

    def spans(step, size, width):
        if step == 0:
            return pl.ds(0, size), pl.ds(width, size)
        if step == 1:
            return pl.ds(size - width, width), pl.ds(0, width)
        return pl.ds(0, width), pl.ds(width + size, width)

    def copies(k, i, j):
        src_l, dst_l = spans(i, lines, LINES)
        src_c, dst_c = spans(j, cols, COLS)
        where = dict(
            device_id=(here[0] + i, here[1] + j), device_id_type=pl.DeviceIdType.MESH
        )
        slot = 3 * (1 - i) + 1 - j
        return (
            pltpu.make_async_remote_copy(
                src_ref=img.at[:, src_l, src_c],
                dst_ref=got.at[:, dst_l, dst_c],
                send_sem=sems.at[0, k],
                recv_sem=sems.at[1, k],
                **where,
            ),
            pltpu.make_async_remote_copy(
                src_ref=par,
                dst_ref=got_par.at[slot],
                send_sem=sems.at[2, k],
                recv_sem=sems.at[3, k],
                **where,
            ),
        )

    for k, (i, j) in enumerate(SIDES):

        @pl.when(inside(i, j))
        def _():
            for copy in copies(k, i, j):
                copy.start()

    out[:, LINES : LINES + lines, COLS : COLS + cols] = img[...]
    out_par[4:5, :] = par[...]
    for k, (i, j) in enumerate(SIDES):

        @pl.when(inside(i, j))
        def _():
            for copy in copies(k, i, j):
                copy.wait_send()

        @pl.when(inside(-i, -j))
        def _():
            for copy in copies(k, i, j):
                copy.wait_recv()

    out[:, :LINES, :] = got[:, :LINES, :]
    out[:, LINES + lines :, :] = got[:, LINES + lines :, :]
    out[:, LINES : LINES + lines, :COLS] = got[:, LINES : LINES + lines, :COLS]
    out[:, LINES : LINES + lines, COLS + cols :] = got[:, LINES : LINES + lines, COLS + cols :]
    for slot in range(9):
        if slot != 4:
            out_par[slot : slot + 1, :] = got_par[slot]


def dot_nt(a, b, **kw):
    return lax.dot_general(a, b, (((1,), (1,)), ((), ())), preferred_element_type=F32, **kw)


def split3(x):
    hi = x.astype(BF16)
    rest = x - hi.astype(F32)
    mid = rest.astype(BF16)
    return hi, mid, (rest - mid.astype(F32)).astype(BF16)


def band(rows, span, base, tab, shift, f):
    gap = lax.broadcasted_iota(jnp.int32, (rows, span), 1) - lax.broadcasted_iota(
        jnp.int32, (rows, span), 0
    )
    gap = gap - (base - (TAPS // 2 - 1) + shift)
    out = jnp.zeros((rows, span), F32)
    for t in range(TAPS):
        out = jnp.where(gap == t, tab[f * TAPS + t], out)
    return out.astype(BF16)


def body(
    nu, nv, par, tab, mask, peaks, ext, ref, lobes, out, patch, amp, win, cen, wts, toep, tmp, tmp2,
    flat, flat2,
):
    chunks = (nv * CHIP + 2 * SEARCH + 127) // 128

    def fact(kind, u, v):
        side_u, side_v = u // nu, v // nv
        spot = (kind * nu + u - side_u * nu) * nv + v - side_v * nv
        return par[3 * (side_u + 1) + side_v + 1, spot]

    for u in range(-1, nu + 1):
        rows = CHIP if 0 <= u < nu else SEARCH
        first = u * CHIP + (CHIP - SEARCH if u < 0 else 0)
        low = (first + LINES - 12) // 16 * 16
        high = min(-(-(first + LINES + rows + 12) // 16) * 16, nu * CHIP + 2 * LINES)
        totals = [None] * chunks
        for v in range(-1, nv + 1):
            begin = max(v * CHIP, -SEARCH)
            end = min(v * CHIP + CHIP, nv * CHIP + SEARCH)
            left = (begin + COLS - 12) // 128 * 128
            right = left + 256
            a = band(rows, high - low, first + LINES - low, tab, fact(0, u, v), fact(2, u, v))
            half = jnp.concatenate(
                [
                    jnp.dot(a, ext[c, low:high, left:right], preferred_element_type=F32)
                    for c in range(2)
                ],
                axis=0,
            ).astype(BF16)
            b = band(
                end - begin, 256, begin + COLS - left, tab, fact(1, u, v), fact(3, u, v)
            )
            spot = begin + SEARCH
            while spot < end + SEARCH:
                m = spot // 128
                stop = min(end + SEARCH, (m + 1) * 128)
                part = b[spot - SEARCH - begin : stop - SEARCH - begin]
                pieces = [part]
                if spot > m * 128:
                    pieces.insert(0, jnp.zeros((spot - m * 128, 256), BF16))
                if stop < m * 128 + 128:
                    pieces.append(jnp.zeros((m * 128 + 128 - stop, 256), BF16))
                piece = jnp.concatenate(pieces, axis=0) if len(pieces) > 1 else part
                term = dot_nt(half, piece)
                totals[m] = term if totals[m] is None else totals[m] + term
                spot = stop
        for m in range(chunks):
            re, im = totals[m][:rows], totals[m][rows:]
            amp[first + SEARCH : first + SEARCH + rows, m * 128 : m * 128 + 128] = (
                jnp.sqrt(re * re + im * im).astype(BF16).astype(F32)
            )

    lane = lax.broadcasted_iota(jnp.int32, (2 * CHIP, 128), 1)
    low_lanes = lane < CHIP
    re = ref[0].astype(F32)
    im = ref[1].astype(F32)
    across = jnp.sqrt(re * re + im * im).astype(BF16).astype(F32).T
    for u in range(nu):
        for v in range(nv):
            n = u * nv + v
            lines = slice(u * CHIP, u * CHIP + 2 * CHIP)
            m = v // 2
            if v % 2 == 0:
                win[n] = amp[lines, m * 128 : m * 128 + 128]
            else:
                win[n] = jnp.where(
                    low_lanes,
                    pltpu.roll(amp[lines, m * 128 : m * 128 + 128], 64, 1),
                    pltpu.roll(amp[lines, m * 128 + 128 : m * 128 + 256], 64, 1),
                )
            wide = u // 2 * 128
            chip = across[v * CHIP : v * CHIP + CHIP, wide : wide + 128]
            if u % 2:
                chip = pltpu.roll(chip, 64, 1)
            keep = low_lanes[:CHIP]
            chip = jnp.where(keep, chip, 0.0)
            mean = jnp.sum(jnp.sum(chip, axis=1, keepdims=True), axis=0, keepdims=True)
            mean = mean * (1.0 / (CHIP * CHIP))
            cen[n] = jnp.where(keep, (chip - mean).astype(BF16).astype(F32), 0.0)

    gap_r = lax.broadcasted_iota(jnp.int32, (CHIP, 128), 1) - lax.broadcasted_iota(
        jnp.int32, (CHIP, 128), 0
    )
    ones_r = jnp.where((gap_r >= 0) & (gap_r < CHIP), 1.0, 0.0).astype(BF16)
    gap_c = lax.broadcasted_iota(jnp.int32, (128, 128), 0) - lane
    ones_c = jnp.where((gap_c >= 0) & (gap_c < CHIP), 1.0, 0.0).astype(BF16)

    def one_chip(n, wts, toep, tmp, tmp2):
        w = win[n]
        for s in range(GROUP):
            shifted = pltpu.roll(w, 128 - s, 1) if s else w
            wts[s * 128 : s * 128 + 128, :] = shifted.astype(BF16)
        centred = cen[n]
        for j in range(CHIP):
            k, s = j // GROUP, j % GROUP
            line = jnp.broadcast_to(centred[j : j + 1, :], (CHIP, 128))
            toep[k * CHIP : k * CHIP + CHIP, s * 128 : s * 128 + 128] = pltpu.roll(
                line, 0, 1, stride=1, stride_axis=0
            ).astype(BF16)
        prod = jnp.dot(toep[...], wts[...], preferred_element_type=F32)
        cross = prod[:CHIP]
        for k in range(1, CHIP // GROUP):
            cross = cross + pltpu.roll(prod[k * CHIP : k * CHIP + CHIP], 128 - k * GROUP, 1)
        energy = jnp.sum(jnp.sum(centred * centred, axis=1, keepdims=True), axis=0, keepdims=True)
        square = w * w
        square_hi = square.astype(BF16)
        square_lo = (square - square_hi.astype(F32)).astype(BF16)
        sums = jnp.dot(
            ones_r,
            jnp.concatenate([w.astype(BF16), square_hi, square_lo], axis=1),
            preferred_element_type=F32,
        )
        terms = split3(sums[:, :128]) + split3(sums[:, 128:256] + sums[:, 256:])
        boxes = jnp.dot(jnp.concatenate(terms, axis=0), ones_c, preferred_element_type=F32)
        box = [boxes[i * CHIP : i * CHIP + CHIP] for i in range(6)]
        total = box[2] + box[1] + box[0]
        squares = box[5] + box[4] + box[3]
        normed = cross / jnp.sqrt(
            energy * (squares - total * total * (1.0 / (CHIP * CHIP))) + EPSILON
        )
        land = (mask[n // nv, n % nv] == 1) & low_lanes[:CHIP]
        surface = jnp.where(land, normed, 0.0)
        tmp[...] = surface
        pairs = tmp[pl.ds(0, 32, stride=2), :] + pltpu.roll(tmp[pl.ds(1, 32, stride=2), :], 64, 1)
        flat[n] = pairs
        lead = SEARCH - (PATCH // 2 - 1)
        lobe_a = pltpu.roll(lobes[...], peaks[0, n // nv, n % nv] + lead, 1)
        lobe_d = pltpu.roll(lobes[...], peaks[1, n // nv, n % nv] + lead, 1)
        near = jnp.dot(
            lobe_a,
            jnp.concatenate([surface, jnp.zeros((CHIP, 128), F32)], axis=0),
            preferred_element_type=F32,
            precision=lax.Precision.HIGHEST,
        )
        tall = jnp.concatenate([lobe_d, jnp.zeros((96, 128), F32)], axis=0)
        tmp2[...] = dot_nt(near, tall, precision=lax.Precision.HIGHEST)
        quads = tmp2[pl.ds(0, 8, stride=4), :]
        for r in range(1, 4):
            quads = quads + pltpu.roll(tmp2[pl.ds(r, 8, stride=4), :], 32 * r, 1)
        flat2[n] = quads

    def one_turn(turn, carry):
        for b in range(turns):
            one_chip(turn * turns + b, wts.at[b], toep.at[b], tmp.at[b], tmp2.at[b])
        return carry

    turns = wts.shape[0]
    lax.fori_loop(0, nu * nv // turns, one_turn, 0)
    for u in range(nu):
        for v in range(nv):
            for m in range(CHIP // 2):
                out[u, v : v + 1, m * 128 : m * 128 + 128] = flat[u * nv + v, m : m + 1, :]
            for m in range(8):
                patch[u, v : v + 1, m * 128 : m * 128 + 128] = flat2[u * nv + v, m : m + 1, :]


def per_device(reference_image, secondary_image, block_shifts, shift_bins, land_mask, coarse_peaks):
    nu, nv = land_mask.shape
    facts = -(-4 * nu * nv // 128) * 128
    smem = pl.BlockSpec(memory_space=pltpu.SMEM)
    vmem = pl.BlockSpec(memory_space=pltpu.VMEM)
    n = nu * nv
    turns = 2 if n % 2 == 0 else 1
    chunks = (nv * CHIP + 2 * SEARCH + 127) // 128
    held = (2, nu * CHIP + 2 * LINES, nv * CHIP + 2 * COLS)

    def halo(*refs):
        exchange(("az", "rg"), *refs)

    par, ext = pl.pallas_call(
        halo,
        out_shape=(
            jax.ShapeDtypeStruct((9, facts), jnp.int32),
            jax.ShapeDtypeStruct(held, BF16),
        ),
        in_specs=[pl.BlockSpec(memory_space=pltpu.HBM)] * 3,
        out_specs=(vmem, vmem),
        scratch_shapes=[
            pltpu.VMEM(block_shifts.shape, jnp.int32),
            pltpu.VMEM(shift_bins.shape, jnp.int32),
            pltpu.VMEM(secondary_image.shape, BF16),
            pltpu.SemaphoreType.DMA((3,)),
            pltpu.VMEM((1, facts), jnp.int32),
            pltpu.VMEM((9, 1, facts), jnp.int32),
            pltpu.VMEM(held, BF16),
            pltpu.SemaphoreType.DMA((4, 8)),
        ],
        compiler_params=pltpu.CompilerParams(
            collective_id=0, has_side_effects=True, vmem_limit_bytes=63 * 1024 * 1024
        ),
    )(block_shifts, shift_bins, secondary_image)

    def kernel(*refs):
        body(nu, nv, *refs)

    return pl.pallas_call(
        kernel,
        out_shape=(
            jax.ShapeDtypeStruct((nu, nv, CHIP * CHIP), F32),
            jax.ShapeDtypeStruct((nu, nv, 4 * OVERS * OVERS), F32),
        ),
        in_specs=[smem] * 4 + [vmem] * 3,
        out_specs=(vmem, vmem),
        scratch_shapes=[
            pltpu.VMEM((nu * CHIP + 2 * SEARCH, chunks * 128), F32),
            pltpu.VMEM((n, 2 * CHIP, 128), F32),
            pltpu.VMEM((n, CHIP, 128), F32),
            pltpu.VMEM((turns, GROUP * 128, 128), BF16),
            pltpu.VMEM((turns, CHIP * CHIP // GROUP, GROUP * 128), BF16),
            pltpu.VMEM((turns, CHIP, 128), F32),
            pltpu.VMEM((turns, 2 * OVERS, 128), F32),
            pltpu.VMEM((n, CHIP // 2, 128), F32),
            pltpu.VMEM((n, 8, 128), F32),
        ],
        compiler_params=pltpu.CompilerParams(vmem_limit_bytes=63 * 1024 * 1024),
    )(
        par,
        jnp.asarray(tap_table()),
        land_mask,
        coarse_peaks,
        ext,
        reference_image,
        jnp.asarray(lobe_table()),
    )


def solution(mesh):
    cut = P(None, "az", "rg")
    return jax.shard_map(
        per_device,
        mesh=mesh,
        in_specs=(cut, cut, cut, cut, P("az", "rg"), cut),
        out_specs=(P("az", "rg", None), P("az", "rg", None)),
        check_vma=False,
    )
```

```python
import jax
import jax.numpy as jnp
import ml_dtypes
import numpy as np
from jax import lax
from jax.experimental import pallas as pl
from jax.experimental.pallas import tpu as pltpu
from jax.sharding import PartitionSpec as P

CHIP = 64
SEARCH = 32
TAPS = 8
NBIN = 16
OVERS = 16
PATCH = 8
LINES = 48
COLS = 128
GROUP = 8
EPSILON = 1e-06
F32, BF16 = jnp.float32, jnp.bfloat16


def lanczos(x):
    return np.where(np.abs(x) < 4, np.sinc(x) * np.sinc(x / 4), 0.0)


def tap_table():
    taps = lanczos(np.arange(TAPS)[None, :] - 3 - np.arange(NBIN)[:, None] / NBIN)
    taps = taps.astype(np.float32).astype(ml_dtypes.bfloat16).astype(np.float32)
    return np.concatenate([np.zeros((1, TAPS), np.float32), taps]).reshape(-1)


def lobe_table():
    at = (np.arange(2 * OVERS) - OVERS) / OVERS
    lobes = lanczos(at[:, None] - (np.arange(PATCH) - (PATCH // 2 - 1))[None, :])
    return np.pad(lobes.astype(np.float32), ((0, 0), (0, 128 - PATCH)))


SIDES = [(i, j) for i in (-1, 0, 1) for j in (-1, 0, 1) if (i, j) != (0, 0)]


def exchange(
    axes, far_shifts, far_bins, far_img, out_par, out, shifts, bins, img, near_sems, par, got_par, got, sems
):
    lines, cols = img.shape[1:]
    here = [lax.axis_index(a) for a in axes]
    count = [lax.axis_size(a) for a in axes]

    def inside(i, j):
        row, col = here[0] + i, here[1] + j
        return (row >= 0) & (row < count[0]) & (col >= 0) & (col < count[1])

    loads = [
        pltpu.make_async_copy(far, near, near_sems.at[k])
        for k, (far, near) in enumerate(
            ((far_img, img), (far_shifts, shifts), (far_bins, bins))
        )
    ]
    for load in loads:
        load.start()
    got[...] = jnp.zeros_like(got)
    got_par[...] = jnp.zeros_like(got_par)
    barrier = pltpu.get_barrier_semaphore()
    for i, j in SIDES:

        @pl.when(inside(i, j))
        def _():
            pl.semaphore_signal(
                barrier,
                inc=1,
                device_id=(here[0] + i, here[1] + j),
                device_id_type=pl.DeviceIdType.MESH,
            )

    tall, wide = (
        1 + jnp.where(h > 0, 1, 0) + jnp.where(h < n - 1, 1, 0) for h, n in zip(here, count)
    )
    for load in loads:
        load.wait()
    rows = [shifts[k, u : u + 1, :] for k in range(2) for u in range(shifts.shape[1])]
    rows += [bins[k, u : u + 1, :] + 1 for k in range(2) for u in range(shifts.shape[1])]
    rest = par.shape[1] - len(rows) * shifts.shape[2]
    if rest:
        rows.append(jnp.zeros((1, rest), jnp.int32))
    par[...] = jnp.concatenate(rows, axis=1)
    pl.semaphore_wait(barrier, tall * wide - 1)

    def spans(step, size, width):
        if step == 0:
            return pl.ds(0, size), pl.ds(width, size)
        if step == 1:
            return pl.ds(size - width, width), pl.ds(0, width)
        return pl.ds(0, width), pl.ds(width + size, width)

    def copies(k, i, j):
        src_l, dst_l = spans(i, lines, LINES)
        src_c, dst_c = spans(j, cols, COLS)
        where = dict(
            device_id=(here[0] + i, here[1] + j), device_id_type=pl.DeviceIdType.MESH
        )
        slot = 3 * (1 - i) + 1 - j
        return (
            pltpu.make_async_remote_copy(
                src_ref=img.at[:, src_l, src_c],
                dst_ref=got.at[:, dst_l, dst_c],
                send_sem=sems.at[0, k],
                recv_sem=sems.at[1, k],
                **where,
            ),
            pltpu.make_async_remote_copy(
                src_ref=par,
                dst_ref=got_par.at[slot],
                send_sem=sems.at[2, k],
                recv_sem=sems.at[3, k],
                **where,
            ),
        )

    for k, (i, j) in enumerate(SIDES):

        @pl.when(inside(i, j))
        def _():
            for copy in copies(k, i, j):
                copy.start()

    out[:, LINES : LINES + lines, COLS : COLS + cols] = img[...]
    out_par[4:5, :] = par[...]
    for k, (i, j) in enumerate(SIDES):

        @pl.when(inside(i, j))
        def _():
            for copy in copies(k, i, j):
                copy.wait_send()

        @pl.when(inside(-i, -j))
        def _():
            for copy in copies(k, i, j):
                copy.wait_recv()

    out[:, :LINES, :] = got[:, :LINES, :]
    out[:, LINES + lines :, :] = got[:, LINES + lines :, :]
    out[:, LINES : LINES + lines, :COLS] = got[:, LINES : LINES + lines, :COLS]
    out[:, LINES : LINES + lines, COLS + cols :] = got[:, LINES : LINES + lines, COLS + cols :]
    for slot in range(9):
        if slot != 4:
            out_par[slot : slot + 1, :] = got_par[slot]


def dot_nt(a, b, **kw):
    return lax.dot_general(a, b, (((1,), (1,)), ((), ())), preferred_element_type=F32, **kw)


def split3(x):
    hi = x.astype(BF16)
    rest = x - hi.astype(F32)
    mid = rest.astype(BF16)
    return hi, mid, (rest - mid.astype(F32)).astype(BF16)


def band(rows, span, base, tab, shift, f):
    gap = lax.broadcasted_iota(jnp.int32, (rows, span), 1) - lax.broadcasted_iota(
        jnp.int32, (rows, span), 0
    )
    gap = gap - (base - (TAPS // 2 - 1) + shift)
    out = jnp.zeros((rows, span), F32)
    for t in range(TAPS):
        out = jnp.where(gap == t, tab[f * TAPS + t], out)
    return out.astype(BF16)


def body(
    nu, nv, par, tab, mask, peaks, ext, ref, lobes, out, patch, amp, win, cen, wts, toep, tmp, tmp2,
    flat, flat2,
):
    chunks = (nv * CHIP + 2 * SEARCH + 127) // 128

    def fact(kind, u, v):
        side_u, side_v = u // nu, v // nv
        spot = (kind * nu + u - side_u * nu) * nv + v - side_v * nv
        return par[3 * (side_u + 1) + side_v + 1, spot]

    for u in range(-1, nu + 1):
        rows = CHIP if 0 <= u < nu else SEARCH
        first = u * CHIP + (CHIP - SEARCH if u < 0 else 0)
        low = (first + LINES - 12) // 16 * 16
        high = min(-(-(first + LINES + rows + 12) // 16) * 16, nu * CHIP + 2 * LINES)
        totals = [None] * chunks
        for v in range(-1, nv + 1):
            begin = max(v * CHIP, -SEARCH)
            end = min(v * CHIP + CHIP, nv * CHIP + SEARCH)
            left = (begin + COLS - 12) // 128 * 128
            right = left + 256
            a = band(rows, high - low, first + LINES - low, tab, fact(0, u, v), fact(2, u, v))
            half = jnp.concatenate(
                [
                    jnp.dot(a, ext[c, low:high, left:right], preferred_element_type=F32)
                    for c in range(2)
                ],
                axis=0,
            ).astype(BF16)
            b = band(
                end - begin, 256, begin + COLS - left, tab, fact(1, u, v), fact(3, u, v)
            )
            spot = begin + SEARCH
            while spot < end + SEARCH:
                m = spot // 128
                stop = min(end + SEARCH, (m + 1) * 128)
                part = b[spot - SEARCH - begin : stop - SEARCH - begin]
                pieces = [part]
                if spot > m * 128:
                    pieces.insert(0, jnp.zeros((spot - m * 128, 256), BF16))
                if stop < m * 128 + 128:
                    pieces.append(jnp.zeros((m * 128 + 128 - stop, 256), BF16))
                piece = jnp.concatenate(pieces, axis=0) if len(pieces) > 1 else part
                term = dot_nt(half, piece)
                totals[m] = term if totals[m] is None else totals[m] + term
                spot = stop
        for m in range(chunks):
            re, im = totals[m][:rows], totals[m][rows:]
            amp[first + SEARCH : first + SEARCH + rows, m * 128 : m * 128 + 128] = (
                jnp.sqrt(re * re + im * im).astype(BF16).astype(F32)
            )

    lane = lax.broadcasted_iota(jnp.int32, (2 * CHIP, 128), 1)
    low_lanes = lane < CHIP
    re = ref[0].astype(F32)
    im = ref[1].astype(F32)
    across = jnp.sqrt(re * re + im * im).astype(BF16).astype(F32).T
    for u in range(nu):
        for v in range(nv):
            n = u * nv + v
            lines = slice(u * CHIP, u * CHIP + 2 * CHIP)
            m = v // 2
            if v % 2 == 0:
                win[n] = amp[lines, m * 128 : m * 128 + 128]
            else:
                win[n] = jnp.where(
                    low_lanes,
                    pltpu.roll(amp[lines, m * 128 : m * 128 + 128], 64, 1),
                    pltpu.roll(amp[lines, m * 128 + 128 : m * 128 + 256], 64, 1),
                )
            wide = u // 2 * 128
            chip = across[v * CHIP : v * CHIP + CHIP, wide : wide + 128]
            if u % 2:
                chip = pltpu.roll(chip, 64, 1)
            keep = low_lanes[:CHIP]
            chip = jnp.where(keep, chip, 0.0)
            mean = jnp.sum(jnp.sum(chip, axis=1, keepdims=True), axis=0, keepdims=True)
            mean = mean * (1.0 / (CHIP * CHIP))
            cen[n] = jnp.where(keep, (chip - mean).astype(BF16).astype(F32), 0.0)

    gap_r = lax.broadcasted_iota(jnp.int32, (CHIP, 128), 1) - lax.broadcasted_iota(
        jnp.int32, (CHIP, 128), 0
    )
    ones_r = jnp.where((gap_r >= 0) & (gap_r < CHIP), 1.0, 0.0).astype(BF16)
    gap_c = lax.broadcasted_iota(jnp.int32, (128, 128), 0) - lane
    ones_c = jnp.where((gap_c >= 0) & (gap_c < CHIP), 1.0, 0.0).astype(BF16)

    def one_chip(n, wts, toep, tmp, tmp2):
        w = win[n]
        for s in range(GROUP):
            shifted = pltpu.roll(w, 128 - s, 1) if s else w
            wts[s * 128 : s * 128 + 128, :] = shifted.astype(BF16)
        centred = cen[n]
        for j in range(CHIP):
            k, s = j // GROUP, j % GROUP
            line = jnp.broadcast_to(centred[j : j + 1, :], (CHIP, 128))
            toep[k * CHIP : k * CHIP + CHIP, s * 128 : s * 128 + 128] = pltpu.roll(
                line, 0, 1, stride=1, stride_axis=0
            ).astype(BF16)
        prod = jnp.dot(toep[...], wts[...], preferred_element_type=F32)
        cross = prod[:CHIP]
        for k in range(1, CHIP // GROUP):
            cross = cross + pltpu.roll(prod[k * CHIP : k * CHIP + CHIP], 128 - k * GROUP, 1)
        energy = jnp.sum(jnp.sum(centred * centred, axis=1, keepdims=True), axis=0, keepdims=True)
        square = w * w
        square_hi = square.astype(BF16)
        square_lo = (square - square_hi.astype(F32)).astype(BF16)
        sums = jnp.dot(
            ones_r,
            jnp.concatenate([w.astype(BF16), square_hi, square_lo], axis=1),
            preferred_element_type=F32,
        )
        terms = split3(sums[:, :128]) + split3(sums[:, 128:256] + sums[:, 256:])
        boxes = jnp.dot(jnp.concatenate(terms, axis=0), ones_c, preferred_element_type=F32)
        box = [boxes[i * CHIP : i * CHIP + CHIP] for i in range(6)]
        total = box[2] + box[1] + box[0]
        squares = box[5] + box[4] + box[3]
        normed = cross / jnp.sqrt(
            energy * (squares - total * total * (1.0 / (CHIP * CHIP))) + EPSILON
        )
        land = (mask[n // nv, n % nv] == 1) & low_lanes[:CHIP]
        surface = jnp.where(land, normed, 0.0)
        tmp[...] = surface
        pairs = tmp[pl.ds(0, 32, stride=2), :] + pltpu.roll(tmp[pl.ds(1, 32, stride=2), :], 64, 1)
        flat[n] = pairs
        lead = SEARCH - (PATCH // 2 - 1)
        lobe_a = pltpu.roll(lobes[...], peaks[0, n // nv, n % nv] + lead, 1)
        lobe_d = pltpu.roll(lobes[...], peaks[1, n // nv, n % nv] + lead, 1)
        near = jnp.dot(
            lobe_a,
            jnp.concatenate([surface, jnp.zeros((CHIP, 128), F32)], axis=0),
            preferred_element_type=F32,
            precision=lax.Precision.HIGHEST,
        )
        tall = jnp.concatenate([lobe_d, jnp.zeros((96, 128), F32)], axis=0)
        tmp2[...] = dot_nt(near, tall, precision=lax.Precision.HIGHEST)
        quads = tmp2[pl.ds(0, 8, stride=4), :]
        for r in range(1, 4):
            quads = quads + pltpu.roll(tmp2[pl.ds(r, 8, stride=4), :], 32 * r, 1)
        flat2[n] = quads

    def one_turn(turn, carry):
        for b in range(turns):
            one_chip(turn * turns + b, wts.at[b], toep.at[b], tmp.at[b], tmp2.at[b])
        return carry

    turns = wts.shape[0]
    lax.fori_loop(0, nu * nv // turns, one_turn, 0)
    for u in range(nu):
        for v in range(nv):
            for m in range(CHIP // 2):
                out[u, v : v + 1, m * 128 : m * 128 + 128] = flat[u * nv + v, m : m + 1, :]
            for m in range(8):
                patch[u, v : v + 1, m * 128 : m * 128 + 128] = flat2[u * nv + v, m : m + 1, :]


def per_device(reference_image, secondary_image, block_shifts, shift_bins, land_mask, coarse_peaks):
    nu, nv = land_mask.shape
    facts = -(-4 * nu * nv // 128) * 128
    smem = pl.BlockSpec(memory_space=pltpu.SMEM)
    vmem = pl.BlockSpec(memory_space=pltpu.VMEM)
    n = nu * nv
    turns = next(t for t in (4, 2, 1) if n % t == 0)
    chunks = (nv * CHIP + 2 * SEARCH + 127) // 128
    held = (2, nu * CHIP + 2 * LINES, nv * CHIP + 2 * COLS)

    def halo(*refs):
        exchange(("az", "rg"), *refs)

    par, ext = pl.pallas_call(
        halo,
        out_shape=(
            jax.ShapeDtypeStruct((9, facts), jnp.int32),
            jax.ShapeDtypeStruct(held, BF16),
        ),
        in_specs=[pl.BlockSpec(memory_space=pltpu.HBM)] * 3,
        out_specs=(vmem, vmem),
        scratch_shapes=[
            pltpu.VMEM(block_shifts.shape, jnp.int32),
            pltpu.VMEM(shift_bins.shape, jnp.int32),
            pltpu.VMEM(secondary_image.shape, BF16),
            pltpu.SemaphoreType.DMA((3,)),
            pltpu.VMEM((1, facts), jnp.int32),
            pltpu.VMEM((9, 1, facts), jnp.int32),
            pltpu.VMEM(held, BF16),
            pltpu.SemaphoreType.DMA((4, 8)),
        ],
        compiler_params=pltpu.CompilerParams(
            collective_id=0, has_side_effects=True, vmem_limit_bytes=63 * 1024 * 1024
        ),
    )(block_shifts, shift_bins, secondary_image)

    def kernel(*refs):
        body(nu, nv, *refs)

    return pl.pallas_call(
        kernel,
        out_shape=(
            jax.ShapeDtypeStruct((nu, nv, CHIP * CHIP), F32),
            jax.ShapeDtypeStruct((nu, nv, 4 * OVERS * OVERS), F32),
        ),
        in_specs=[smem] * 4 + [vmem] * 3,
        out_specs=(vmem, vmem),
        scratch_shapes=[
            pltpu.VMEM((nu * CHIP + 2 * SEARCH, chunks * 128), F32),
            pltpu.VMEM((n, 2 * CHIP, 128), F32),
            pltpu.VMEM((n, CHIP, 128), F32),
            pltpu.VMEM((turns, GROUP * 128, 128), BF16),
            pltpu.VMEM((turns, CHIP * CHIP // GROUP, GROUP * 128), BF16),
            pltpu.VMEM((turns, CHIP, 128), F32),
            pltpu.VMEM((turns, 2 * OVERS, 128), F32),
            pltpu.VMEM((n, CHIP // 2, 128), F32),
            pltpu.VMEM((n, 8, 128), F32),
        ],
        compiler_params=pltpu.CompilerParams(vmem_limit_bytes=63 * 1024 * 1024),
    )(
        par,
        jnp.asarray(tap_table()),
        land_mask,
        coarse_peaks,
        ext,
        reference_image,
        jnp.asarray(lobe_table()),
    )


def solution(mesh):
    cut = P(None, "az", "rg")
    return jax.shard_map(
        per_device,
        mesh=mesh,
        in_specs=(cut, cut, cut, cut, P("az", "rg"), cut),
        out_specs=(P("az", "rg", None), P("az", "rg", None)),
        check_vma=False,
    )
```
